32 devices in a mesh: dp: 16 (over z, x, core), group: 2 (over y).
Axes of the slice: x: 2, y: 2, z: 4, core: 2. Of those that a mesh axis runs over, the one named last changes fastest.
Arguments:
- tokens: bfloat16 [16384, 768], P(('dp', 'group')), may hold values from -6 to 6
- lengths: int32 [16], P('dp'), may hold values from 512 to 1024, as said below
- cotangent: bfloat16 [16384, 768], P(('dp', 'group')), may hold values from -6 to 6
- w_query: bfloat16 [768, 768], replicated, may hold values from -0.109375 to 0.109375
- w_keys: bfloat16 [768, 768], replicated, may hold values from -0.109375 to 0.109375
- w_values: bfloat16 [768, 768], replicated, may hold values from -0.21875 to 0.21875
- w_output: bfloat16 [768, 768], replicated, may hold values from -1.25 to 1.25
- w_gate: bfloat16 [768, 2048], replicated, may hold values from -0.21875 to 0.21875
- w_up: bfloat16 [768, 2048], replicated, may hold values from -0.21875 to 0.21875
- w_down: bfloat16 [2048, 768], replicated, may hold values from -0.1875 to 0.1875
- gain_attn: bfloat16 [768], replicated, may hold values from 0.5 to 1.5
- gain_ffn: bfloat16 [768], replicated, may hold values from 0.5 to 1.5
- bias_table: bfloat16 [32, 12], replicated, may hold values from -3 to 3
- master: float32 [55328, 128], P(('dp', 'group')), may hold values from -0.15625 to 0.15625
- moment_one: float32 [55328, 128], P(('dp', 'group')), may hold values from -64 to 64
- moment_two: float32 [55328, 128], P(('dp', 'group')), may hold values from 1 to 10000
Outputs:
- layer_out: bfloat16 [16384, 768], P(('dp', 'group'))
- grad_tokens: float32 [16384, 768], P(('dp', 'group'))
- grad_flat: float32 [55328, 128], P(('dp', 'group'))
- moment_one_new: float32 [55328, 128], P(('dp', 'group'))
- moment_two_new: float32 [55328, 128], P(('dp', 'group'))
- master_new: float32 [55328, 128], P(('dp', 'group'))
- fresh_copy: bfloat16 [55328, 128], replicated
The draws below stay inside these ranges and needn't reach their ends.
Inputs may be any that keep to these rules, and one draw needn't show every extreme that they name: `lengths`: each slot's live tokens are a prefix of it; some slot is full.
All inputs are finite; a program needn't handle non-finite values.
Results may differ from the reference program's by a relative error of at most 0.015.
The reference program's roundings to bfloat16 on the way count: a program that leaves them out, or rounds other values in their place, can miss the bound.
Values may be sent and summed in bfloat16 or wider, within the bound.
A program may use at most 320 MiB of HBM per device.

```python
import math
import jax
import jax.numpy as jnp
import numpy as np
from jax import lax

D = 768
FF = 2048
HEADS = 12
HEAD_DIM = 64
BUCKETS = 32
LEN_MIN = 512
SLOT = 1024
SLOTS = 16
TOKENS = 16384
FLAT_ROWS = 55328


def draw_lengths(key, part):
    first_key, second_key = jax.random.split(jax.random.fold_in(key, 17))
    drawn = jax.random.randint(first_key, (SLOTS,), LEN_MIN, SLOT + 1)
    fullest = jax.random.randint(second_key, (), 0, SLOTS)
    return jnp.where(jnp.arange(SLOTS) == fullest, SLOT, drawn).astype(jnp.int32)


def block_scale(own_key, dims, cuts, smallest, largest):
    def one(position, blocks):
        draws = jax.random.uniform(jax.random.fold_in(jax.random.fold_in(own_key, 6), position), (blocks,), jnp.float32, smallest / len(cuts), largest / len(cuts))
        return jnp.repeat(jnp.exp(draws), dims[position] // blocks).reshape((-1,) + (1,) * (len(dims) - position - 1))

    loudness = one(*cuts[0])
    for cut in cuts[1:]:
        loudness = loudness * one(*cut)
    return loudness


def bell_draw(rng, dims, deviation, most, cuts=(), kind=jnp.bfloat16):
    gain = block_scale(rng, dims, cuts, -0.22, 0.18) if cuts else 1.0
    result = jax.random.normal(rng, dims, jnp.float32) * deviation * gain
    return jnp.minimum(jnp.maximum(result, -most), most).astype(kind)


def setup_inputs(seed: int = 0) -> dict:
    seeds = jax.random.split(jax.random.key(seed), 17)
    tokens = bell_draw(seeds[0], (TOKENS, D), 1.0, 6.0, ((0, 32),))
    lengths = draw_lengths(jax.random.fold_in(seeds[16], 71), 0)
    cotangent = bell_draw(seeds[2], (TOKENS, D), 1.0, 6.0, ((0, 32),))
    w_query = bell_draw(seeds[3], (D, D), (4 * D) ** -0.5, 0.109375)
    w_keys = bell_draw(seeds[4], (D, D), (4 * D) ** -0.5, 0.109375)
    w_values = bell_draw(seeds[5], (D, D), D ** -0.5, 0.21875)
    w_output = bell_draw(seeds[6], (D, D), (D // 32) ** -0.5, 1.25)
    w_gate = bell_draw(seeds[7], (D, FF), D ** -0.5, 0.21875)
    w_up = bell_draw(seeds[8], (D, FF), D ** -0.5, 0.21875)
    w_down = bell_draw(seeds[9], (FF, D), (FF // 2) ** -0.5, 0.1875)
    gain_attn = jnp.clip(1.0 + 0.1 * jax.random.normal(seeds[10], (D,), jnp.float32), 0.5, 1.5).astype(jnp.bfloat16)
    gain_ffn = jnp.clip(1.0 + 0.1 * jax.random.normal(seeds[11], (D,), jnp.float32), 0.5, 1.5).astype(jnp.bfloat16)
    bias_table = bell_draw(seeds[12], (BUCKETS, HEADS), 0.5, 3.0)
    master = bell_draw(seeds[13], (FLAT_ROWS, 128), 0.01, 0.15625, ((0, 32),), jnp.float32)
    moment_one = bell_draw(seeds[14], (FLAT_ROWS, 128), 10.0, 64.0, ((0, 32),), jnp.float32)
    moment_two = jnp.clip(jnp.exp(math.log(10000.0) - 9.2103404 * jax.random.uniform(seeds[15], (FLAT_ROWS, 128), jnp.float32) ** block_scale(seeds[15], (FLAT_ROWS, 128), ((0, 32),), -0.2, 0.2)), 1.0, 10000.0)
    return dict(tokens=tokens, lengths=lengths, cotangent=cotangent, w_query=w_query, w_keys=w_keys, w_values=w_values, w_output=w_output, w_gate=w_gate, w_up=w_up, w_down=w_down, gain_attn=gain_attn, gain_ffn=gain_ffn, bias_table=bias_table, master=master, moment_one=moment_one, moment_two=moment_two)


@jax.custom_vjp
def low(v):
    return lax.optimization_barrier(v.astype(jnp.bfloat16)).astype(jnp.float32)

@jax.custom_vjp
def low_back(v):
    return v

def low_keep(v):
    return (low(v), None)

def low_pass(kept, grad):
    return (grad,)

def back_keep(v):
    return (v, None)

def back_low(kept, grad):
    return (low(grad),)
low.defvjp(low_keep, low_pass)
low_back.defvjp(back_keep, back_low)
far_steps = np.array([8, 12, 16, 23, 32, 46, 64, 91], dtype=np.int32)

def bucket_index(offset):
    distance = jnp.abs(offset)
    passed = lax.optimization_barrier(jnp.sum((distance[..., None] >= far_steps).astype(jnp.int32), axis=-1))
    inside = jnp.where(distance < 8, distance, 7 + passed)
    return (inside + 16 * (offset > 0).astype(jnp.int32)).astype(jnp.int32)

def rms_scale(values_in, gain_in):
    return values_in * lax.rsqrt(lax.optimization_barrier(jnp.mean(values_in * values_in, axis=-1, keepdims=True)) + 1e-06) * gain_in

def gelu_tanh(values_in):
    return 0.5 * values_in * (1.0 + jnp.tanh(0.7978845608028654 * (values_in + 0.044715 * values_in * values_in * values_in)))

def slot_forward(params, slot_tokens, slot_length):
    w_query, w_keys, w_values, w_output, w_gate, w_up, w_down, gain_attn, gain_ffn, bias_table = params
    highest = lax.Precision.HIGHEST
    normed = low(rms_scale(slot_tokens, gain_attn))
    query_rows = low(low_back(jnp.dot(normed, w_query, precision=highest)))
    key_rows = low(low_back(jnp.dot(normed, w_keys, precision=highest)))
    value_rows = low(low_back(jnp.dot(normed, w_values, precision=highest)))
    query_heads = query_rows.reshape(SLOT, HEADS, HEAD_DIM)
    key_heads = key_rows.reshape(SLOT, HEADS, HEAD_DIM)
    value_heads = value_rows.reshape(SLOT, HEADS, HEAD_DIM)
    places = jnp.arange(SLOT, dtype=jnp.int32)
    buckets = bucket_index(places[None, :] - places[:, None])
    rel_bias = jnp.transpose(bias_table[buckets], (2, 0, 1))
    scores = jnp.einsum('qhd,khd->hqk', query_heads, key_heads, precision=highest) + rel_bias
    scores = low_back(scores)
    key_live = places < slot_length
    scores = jnp.where(key_live[None, None, :], scores, -jnp.inf)
    prob_low = low(jax.nn.softmax(scores, axis=-1))
    mixed = jnp.einsum('hqk,khd->qhd', prob_low, value_heads, precision=highest).reshape(SLOT, D)
    mixed = low(low_back(mixed))
    branch = low_back(jnp.dot(mixed, w_output, precision=highest))
    hidden_state = slot_tokens + branch
    normed_ffn = low(rms_scale(hidden_state, gain_ffn))
    gate_act = low_back(jnp.dot(normed_ffn, w_gate, precision=highest))
    up_act = low_back(jnp.dot(normed_ffn, w_up, precision=highest))
    inner_act = low(gelu_tanh(gate_act) * up_act)
    ffn_branch = low_back(jnp.dot(inner_act, w_down, precision=highest))
    return hidden_state + ffn_branch

def reference(tokens, lengths, cotangent, w_query, w_keys, w_values, w_output, w_gate, w_up, w_down, gain_attn, gain_ffn, bias_table, master, moment_one, moment_two):
    params = tuple((member.astype(jnp.float32) for member in (w_query, w_keys, w_values, w_output, w_gate, w_up, w_down, gain_attn, gain_ffn, bias_table)))
    slot_inputs = tokens.astype(jnp.float32).reshape(SLOTS, SLOT, D)
    slot_cots = cotangent.astype(jnp.float32).reshape(SLOTS, SLOT, D)
    places = jnp.arange(SLOT, dtype=jnp.int32)

    def one_slot(grad_sum, slot_item):
        slot_tokens, slot_cot, slot_length = slot_item
        outputs, pull_back = jax.vjp(lambda weights, inputs: slot_forward(weights, inputs, slot_length), params, slot_tokens)
        live = (places < slot_length).astype(slot_cot.dtype)[:, None]
        grad_params, grad_inputs = pull_back(slot_cot * live)
        grad_sum = jax.tree.map(lambda first, second: first + second, grad_sum, grad_params)
        return (grad_sum, (outputs.astype(jnp.bfloat16), grad_inputs))
    zero_grads = tuple((jnp.zeros_like(member) for member in params))
    grads, (slot_outputs, slot_grads) = lax.scan(one_slot, zero_grads, (slot_inputs, slot_cots, lengths))
    flat_grads = jnp.concatenate([member.reshape(-1) for member in grads])
    flat_grads = jnp.pad(flat_grads, (0, FLAT_ROWS * 128 - flat_grads.shape[0])).reshape(FLAT_ROWS, 128)
    moment_one_new = 0.9 * moment_one + 0.1 * flat_grads
    moment_two_new = 0.999 * moment_two + 0.001 * flat_grads * flat_grads
    first_hat = moment_one_new / (1.0 - 0.9 ** 10)
    second_hat = moment_two_new / (1.0 - 0.999 ** 10)
    master_new = master - 0.01 * (first_hat / (jnp.sqrt(second_hat) + 1e-08) + 0.1 * master)
    fresh_copy = master_new.astype(jnp.bfloat16)
    return (slot_outputs.reshape(TOKENS, D), slot_grads.reshape(TOKENS, D), flat_grads, moment_one_new, moment_two_new, master_new, fresh_copy)
```

```python
import functools
import jax
import jax.numpy as jnp
import numpy as np
from jax import lax
from jax.experimental import pallas as pl
from jax.experimental.pallas import tpu as pltpu
from jax.sharding import PartitionSpec as P

MESH = pl.DeviceIdType.MESH
bf16, f32 = jnp.bfloat16, jnp.float32


class Grid:
    def __init__(self, dp):
        half = dp // 2
        self.X = 1
        while self.X * self.X * 4 <= half:
            self.X *= 2
        self.planes = half // self.X
        self.devices = dp * 2
        self.swap = self.X == 2

    def here(self):
        dp = lax.axis_index("dp")
        self.core = lax.rem(dp, 2)
        self.x = lax.rem(dp // 2, self.X)
        self.plane = dp // (2 * self.X)
        self.y = lax.axis_index("group")
        self.flip = self.core if self.swap else 0
        if self.swap:
            self.a = jnp.where(self.core == 0, self.x, self.y)
            self.b = jnp.where(self.core == 0, self.y, self.x)
        else:
            self.a, self.b = self.x, self.y
        return self

    def xy(self, a, b):
        if not self.swap:
            return a, b
        return jnp.where(self.core == 0, a, b), jnp.where(self.core == 0, b, a)

    def device(self, plane=None, a=None, b=None, core=None):
        plane = self.plane if plane is None else plane
        a = self.a if a is None else a
        b = self.b if b is None else b
        x, y = self.xy(a, b)
        core = self.core if core is None else core
        return ((plane * self.X + x) * 2 + core, y)

    def index(self, plane, x, core, y):
        return ((plane * self.X + x) * 2 + core) * 2 + y

    def partners(self):
        found = [self.device(core=1 - self.core), self.device(b=1 - self.b)]
        found += [self.device(a=lax.rem(self.a + d, self.X)) for d in range(1, self.X)]
        found += [self.device(plane=lax.rem(self.plane + d, self.planes)) for d in range(1, self.planes)]
        return found


def enter(partners):
    barrier = pltpu.get_barrier_semaphore()
    for one in partners:
        pl.semaphore_signal(barrier, inc=1, device_id=one, device_id_type=MESH)
    pl.semaphore_wait(barrier, len(partners))


def add_rows(out, terms, rows, block):
    @pl.loop(0, rows // block)
    def _(step):
        part = pl.ds(pl.multiple_of(step * block, block), block)
        total = terms[0][part, :].astype(f32)
        for term in terms[1:]:
            total = total + term[part, :].astype(f32)
        out[part, :] = total.astype(out.dtype)


def block_of(rows):
    for tiles in range(12, 0, -1):
        if rows % (16 * tiles) == 0:
            return 16 * tiles


class Scatter:
    def __init__(self, grid, first, count, stride, window):
        self.g, self.first, self.count, self.stride, self.window = grid, first, count, stride, window

    def scratch(self):
        g, n, w = self.g, self.count, self.window
        dma = pltpu.SemaphoreType.DMA
        return [
            pltpu.VMEM((n, g.X, 2, w, 128), bf16),
            pltpu.VMEM((n, g.X, 2, w, 128), bf16),
            pltpu.VMEM((n, g.X - 1, 2, w, 128), bf16),
            pltpu.VMEM((n, w, 128), bf16),
            pltpu.VMEM((g.planes - 1, w, 128), bf16),
            pltpu.VMEM((w, 128), bf16),
            dma((n, g.X, 2)), dma((n, g.X, 2)), dma((n, g.X, 2)),
            dma((n, g.X - 1, 2)), dma((n, g.X - 1, 2)),
            dma((n,)), dma((n,)), dma((n,)), dma((g.planes - 1,)),
        ]

    def bind(self, flat, out, scratch):
        (self.own, self.r1, self.r2, self.r3, self.r4, self.kept, self.lsem, self.s1, self.q1, self.s2,
         self.q2, self.s3, self.q3, self.s4, self.q4) = scratch
        self.flat, self.out = flat, out

    def plane_of(self, k):
        return self.first + lax.rem(self.g.plane + 1 + k, self.count)

    def copies0(self, k):
        g = self.g
        q = self.plane_of(k)
        for x in range(g.X):
            for y in range(2):
                there = pl.multiple_of(self.stride * g.index(q, x, 1 - g.core, y), 16)
                here = pl.multiple_of(self.stride * g.index(q, x, g.core, y), 16)
                yield (
                    pltpu.make_async_remote_copy(
                        self.flat.at[pl.ds(there, self.window), :], self.r1.at[k, x, y],
                        self.s1.at[k, x, y], self.q1.at[k, x, y],
                        device_id=g.device(core=1 - g.core), device_id_type=MESH),
                    pltpu.make_async_copy(
                        self.flat.at[pl.ds(here, self.window), :], self.own.at[k, x, y], self.lsem.at[k, x, y]),
                    x, y)

    def copies1(self, k):
        g = self.g
        for d in range(1, g.X):
            a = lax.rem(g.a + d, g.X)
            for b in range(2):
                x, y = g.xy(a, b)
                yield pltpu.make_async_remote_copy(
                    self.own.at[k, x, y], self.r2.at[k, d - 1, b], self.s2.at[k, d - 1, b], self.q2.at[k, d - 1, b],
                    device_id=g.device(a=a), device_id_type=MESH)

    def copy2(self, k):
        g = self.g
        x, y = g.xy(g.a, 1 - g.b)
        return pltpu.make_async_remote_copy(
            self.own.at[k, x, y], self.r3.at[k], self.s3.at[k], self.q3.at[k],
            device_id=g.device(b=1 - g.b), device_id_type=MESH)

    def copy3(self, k):
        g = self.g
        q = self.plane_of(k)
        slot = lax.rem(g.plane - q + g.planes, g.planes) - 1
        slot = jnp.maximum(slot, 0)
        return pltpu.make_async_remote_copy(
            self.own.at[k, g.x, g.y], self.r4.at[slot], self.s4.at[k], self.q4.at[slot],
            device_id=g.device(plane=q), device_id_type=MESH)

    def step(self, stage, k):
        g = self.g
        block = block_of(self.window)
        if stage == 0:
            for far, near, x, y in self.copies0(k):
                far.start()
                near.start()
        elif stage == 1:
            for far, near, x, y in self.copies0(k):
                near.wait()
                far.wait()
                add_rows(self.own.at[k, x, y], [self.own.at[k, x, y], self.r1.at[k, x, y]], self.window, block)
            for copy in self.copies1(k):
                copy.start()
        elif stage == 2:
            for copy in self.copies1(k):
                copy.wait()
            for b in range(2):
                x, y = g.xy(g.a, b)
                mine = self.own.at[k, x, y]
                add_rows(mine, [mine] + [self.r2.at[k, d, b] for d in range(g.X - 1)], self.window, block)
            self.copy2(k).start()
        elif stage == 3:
            self.copy2(k).wait()
            mine = self.own.at[k, g.x, g.y]
            q = self.plane_of(k)
            add_rows(mine, [mine, self.r3.at[k]], self.window, block)

            @pl.when(q != g.plane)
            def _():
                self.copy3(k).start()

            @pl.when(q == g.plane)
            def _():
                add_rows(self.kept, [mine], self.window, block)

    def finish(self):
        g = self.g
        for k in range(self.count):
            @pl.when(self.plane_of(k) != g.plane)
            def _():
                self.copy3(k).wait_send()

        inside = jnp.logical_and(g.plane >= self.first, g.plane < self.first + self.count)

        @pl.when(inside)
        def _():
            for d in range(g.planes - 1):
                pltpu.make_async_remote_copy(
                    self.kept, self.r4.at[d], self.s4.at[0], self.q4.at[d],
                    device_id=g.device(plane=lax.rem(g.plane + 1 + d, g.planes)), device_id_type=MESH).wait_recv()
            add_rows(self.out, [self.kept] + [self.r4.at[d] for d in range(g.planes - 1)], self.window,
                     block_of(self.window))

        @pl.when(jnp.logical_not(inside))
        def _():
            self.out[...] = jnp.zeros_like(self.out)

    def all(self):
        for k in range(self.count):
            self.step(0, k)
        for t in range(self.count + 2):
            for stage in (3, 2, 1):
                k = t - (stage - 1)
                if 0 <= k < self.count:
                    self.step(stage, k)
        self.finish()


def scatter_kernel(grid, make, flat, out, *scratch):
    grid.here()
    enter(grid.partners())
    job = make()
    job.bind(flat, out, scratch)
    job.all()


def scatter_rows(flat, grid, first, count, stride, window, collective_id):
    make = lambda: Scatter(grid, first, count, stride, window)
    return pl.pallas_call(
        functools.partial(scatter_kernel, grid, make),
        out_shape=jax.ShapeDtypeStruct((window, 128), f32),
        in_specs=[pl.BlockSpec(memory_space=pl.ANY)],
        out_specs=pl.BlockSpec(memory_space=pltpu.VMEM),
        scratch_shapes=make().scratch(),
        compiler_params=pltpu.CompilerParams(
            collective_id=collective_id, has_side_effects=True, vmem_limit_bytes=56 << 20),
    )(flat)


def gather_kernel(grid, stride, fresh, tail, out, lsem, tsem, s0, q0, s1, q1, s2, q2, s3, q3):
    g = grid.here()
    enter(g.partners())
    X, planes = g.X, g.planes

    def rows(q, x, core, y):
        return out.at[pl.ds(pl.multiple_of(stride * g.index(q, x, core, y), 16), stride), :]

    mine = rows(g.plane, g.x, g.core, g.y)
    first = pltpu.make_async_copy(fresh, mine, lsem)
    first.start()
    rest = pltpu.make_async_copy(tail, out.at[pl.ds(stride * g.devices, g.devices), :], tsem)
    rest.start()

    def send0(d):
        return pltpu.make_async_remote_copy(
            fresh, mine, s0.at[d - 1], q0.at[d - 1],
            device_id=g.device(plane=lax.rem(g.plane + d, planes)), device_id_type=MESH)

    def plane_of(k):
        return lax.rem(g.plane - k + planes, planes)

    def send1(k):
        part = rows(plane_of(k), g.x, g.core, g.y)
        return pltpu.make_async_remote_copy(
            part, part, s1.at[k], q1.at[k], device_id=g.device(b=1 - g.b), device_id_type=MESH)

    def send2(k):
        for d in range(1, X):
            for b in range(2):
                x, y = g.xy(g.a, b)
                part = rows(plane_of(k), x, g.core, y)
                yield pltpu.make_async_remote_copy(
                    part, part, s2.at[k, d - 1, b], q2.at[k, d - 1, b],
                    device_id=g.device(a=lax.rem(g.a + d, X)), device_id_type=MESH)

    def send3(k):
        for x in range(X):
            for y in range(2):
                part = rows(plane_of(k), x, g.core, y)
                yield pltpu.make_async_remote_copy(
                    part, part, s3.at[k, x, y], q3.at[k, x, y],
                    device_id=g.device(core=1 - g.core), device_id_type=MESH)

    for d in range(1, planes):
        send0(d).start()
    first.wait()
    for t in range(planes + 2):
        if t < planes:
            if t > 0:
                send0(t).wait_recv()
            send1(t).start()
        k = t - 1
        if 0 <= k < planes:
            send1(k).wait_recv()
            for copy in send2(k):
                copy.start()
        k = t - 2
        if 0 <= k < planes:
            for copy in send2(k):
                copy.wait_recv()
            for copy in send3(k):
                copy.start()
    for k in range(planes):
        for copy in send3(k):
            copy.wait_recv()
    for d in range(1, planes):
        send0(d).wait_send()
    for k in range(planes):
        send1(k).wait_send()
        for copy in send2(k):
            copy.wait_send()
        for copy in send3(k):
            copy.wait_send()
    rest.wait()


def gather_rows(fresh, tail, grid, stride, collective_id):
    dma = pltpu.SemaphoreType.DMA
    n, X = grid.planes, grid.X
    total = (stride + 1) * grid.devices
    return pl.pallas_call(
        functools.partial(gather_kernel, grid, stride),
        out_shape=jax.ShapeDtypeStruct((total, 128), bf16),
        in_specs=[pl.BlockSpec(memory_space=pl.ANY)] * 2,
        out_specs=pl.BlockSpec(memory_space=pl.ANY),
        scratch_shapes=[dma, dma, dma((n - 1,)), dma((n - 1,)), dma((n,)), dma((n,)),
                        dma((n, X - 1, 2)), dma((n, X - 1, 2)), dma((n, X, 2)), dma((n, X, 2))],
        compiler_params=pltpu.CompilerParams(collective_id=collective_id, has_side_effects=True),
    )(fresh, tail)


far_steps = np.array([8, 12, 16, 23, 32, 46, 64, 91], dtype=np.int32)
root_half = 0.7978845608028654


def bucket_index(offset):
    distance = jnp.abs(offset)
    passed = jnp.sum((distance[:, None] >= far_steps[None, :]).astype(jnp.int32), axis=1)
    inside = jnp.where(distance < 8, distance, 7 + passed)
    return inside + 16 * (offset > 0).astype(jnp.int32)


def rms_scale(values_in, gain_in):
    return (
        values_in
        * lax.rsqrt(jnp.mean(values_in * values_in, axis=-1, keepdims=True) + 1e-06)
        * gain_in
    )


def gelu_tanh(values_in):
    return (
        0.5
        * values_in
        * (1.0 + jnp.tanh(root_half * (values_in + 0.044715 * values_in * values_in * values_in)))
    )


def gated_product(gate_in, up_in):
    return gelu_tanh(gate_in) * up_in


def matmul(left_op, right_op):
    return jnp.dot(left_op, right_op, preferred_element_type=jnp.float32)


def product_tn(left_op, right_op):
    return lax.dot_general(
        left_op, right_op, (((0,), (0,)), ((), ())), preferred_element_type=jnp.float32
    )


def product_nt(left_op, right_op):
    return lax.dot_general(
        left_op, right_op, (((1,), (1,)), ((), ())), preferred_element_type=jnp.float32
    )


def skew_bias(table_wide, start_pos, block_rows, slot_span):
    width_all = block_rows + slot_span
    offsets = jnp.arange(width_all, dtype=jnp.int32) - (block_rows - 1) - start_pos
    buckets = bucket_index(offsets)
    onehot = (buckets[:, None] == jnp.arange(table_wide.shape[0], dtype=jnp.int32)[None, :]).astype(
        jnp.float32
    )
    per_offset = jnp.sum(onehot[:, :, None] * table_wide[None, :, :], axis=1)
    repeated = jnp.tile(per_offset.T, (1, block_rows))
    window = lax.slice_in_dim(
        repeated, block_rows - 1, block_rows - 1 + block_rows * (width_all - 1), axis=1
    )
    return (
        window.reshape(table_wide.shape[1], block_rows, width_all - 1)[:, :, :slot_span],
        onehot,
    )


def skew_grad(grad_scores, onehot, block_rows, slot_span):
    head_count = grad_scores.shape[0]
    width_all = block_rows + slot_span
    padded = jnp.pad(grad_scores, ((0, 0), (0, 0), (0, block_rows - 1)))
    flat_rows = padded.reshape(head_count, block_rows * (width_all - 1))
    flat_rows = jnp.pad(flat_rows, ((0, 0), (block_rows - 1, 1)))
    per_offset = jnp.sum(
        flat_rows.reshape(head_count, block_rows, width_all), axis=1, dtype=jnp.float32
    )
    return jnp.sum(onehot[:, :, None] * per_offset.T[:, None, :], axis=0)


def block_scores(query_block, key_heads, rel_bias, key_live):
    scores = (
        jnp.einsum("qhd,khd->hqk", query_block, key_heads, preferred_element_type=jnp.float32)
        + rel_bias
    )
    return jnp.where(key_live[None, None, :], scores, -jnp.inf)


def adam_step(grads, moment_one, moment_two, master):
    moment_one_new = 0.9 * moment_one + 0.1 * grads
    moment_two_new = 0.999 * moment_two + 0.001 * grads * grads
    first_hat = moment_one_new / (1.0 - 0.9**10)
    second_hat = moment_two_new / (1.0 - 0.999**10)
    master_new = master - 0.01 * (first_hat / (jnp.sqrt(second_hat) + 1e-08) + 0.1 * master)
    return moment_one_new, moment_two_new, master_new


def per_device(
    tokens,
    lengths,
    cotangent,
    w_query,
    w_keys,
    w_values,
    w_output,
    w_gate,
    w_up,
    w_down,
    gain_attn,
    gain_ffn,
    bias_table,
    master,
    moment_one,
    moment_two,
):
    local_rows, width = tokens.shape
    head_count = bias_table.shape[1]
    head_size = width // head_count
    group_size = lax.axis_size("group")
    slot_span = local_rows * group_size
    live_length = lengths[0]
    first_row = lax.axis_index("group") * local_rows
    block_rows = min(512, local_rows)
    key_live = jnp.arange(slot_span, dtype=jnp.int32) < live_length
    row_live = first_row + jnp.arange(local_rows, dtype=jnp.int32) < live_length
    table_wide = bias_table.astype(jnp.float32)
    inputs_wide = tokens.astype(jnp.float32)
    normed, attn_norm_pull = jax.vjp(rms_scale, inputs_wide, gain_attn.astype(jnp.float32))
    normed_low = normed.astype(jnp.bfloat16)
    query_rows = matmul(normed_low, w_query).astype(jnp.bfloat16)
    key_rows = matmul(normed_low, w_keys).astype(jnp.bfloat16)
    value_rows = matmul(normed_low, w_values).astype(jnp.bfloat16)
    all_keys, all_values = (
        lax.all_gather(key_rows, "group", axis=0, tiled=True),
        lax.all_gather(value_rows, "group", axis=0, tiled=True),
    )
    key_heads = all_keys.reshape(slot_span, head_count, head_size)
    value_heads = all_values.reshape(slot_span, head_count, head_size)
    query_heads = query_rows.reshape(local_rows, head_count, head_size)
    block_id = 0
    row_start = block_id * block_rows
    rel_bias, onehot = skew_bias(table_wide, first_row + row_start, block_rows, slot_span)
    scores = block_scores(query_heads, key_heads, rel_bias, key_live)
    row_max = jnp.max(scores, axis=2, keepdims=True)
    row_total = jnp.sum(jnp.exp(scores - row_max), axis=2, keepdims=True)
    log_total = row_max + jnp.log(row_total)
    prob_low = jnp.exp(scores - log_total).astype(jnp.bfloat16)
    mixed_blocks = jnp.einsum(
        "hqk,khd->qhd", prob_low, value_heads, preferred_element_type=jnp.float32
    )
    log_totals = [log_total]
    mixed_low = mixed_blocks.reshape(local_rows, width).astype(jnp.bfloat16)
    hidden_state = inputs_wide + matmul(mixed_low, w_output)
    normed_ffn, ffn_norm_pull = jax.vjp(rms_scale, hidden_state, gain_ffn.astype(jnp.float32))
    normed_ffn_low = normed_ffn.astype(jnp.bfloat16)
    gate_act = matmul(normed_ffn_low, w_gate)
    up_act = matmul(normed_ffn_low, w_up)
    inner_act, gated_pull = jax.vjp(gated_product, gate_act, up_act)
    inner_low = inner_act.astype(jnp.bfloat16)
    layer_out = (hidden_state + matmul(inner_low, w_down)).astype(jnp.bfloat16)
    grad_out = jnp.where(row_live[:, None], cotangent, jnp.zeros_like(cotangent))
    grad_w_down = product_tn(inner_low, grad_out)
    grad_inner = product_nt(grad_out, w_down)
    grad_gate, grad_up = gated_pull(grad_inner)
    grad_gate_low = grad_gate.astype(jnp.bfloat16)
    grad_up_low = grad_up.astype(jnp.bfloat16)
    grad_w_gate = product_tn(normed_ffn_low, grad_gate_low)
    grad_w_up = product_tn(normed_ffn_low, grad_up_low)
    grad_normed_ffn = product_nt(grad_gate_low, w_gate) + product_nt(grad_up_low, w_up)
    grad_from_norm, grad_gain_ffn = ffn_norm_pull(grad_normed_ffn)
    grad_hidden = grad_out.astype(jnp.float32) + grad_from_norm
    grad_branch = grad_hidden.astype(jnp.bfloat16)
    grad_w_output = product_tn(mixed_low, grad_branch)
    grad_mixed = product_nt(grad_branch, w_output).astype(jnp.bfloat16)
    grad_mixed_heads = grad_mixed.reshape(local_rows, head_count, head_size)
    block_id = 0
    row_start = block_id * block_rows
    rel_bias, onehot = skew_bias(table_wide, first_row + row_start, block_rows, slot_span)
    scores = block_scores(query_heads, key_heads, rel_bias, key_live)
    prob_full = jnp.exp(scores - log_totals[block_id])
    prob_low = prob_full.astype(jnp.bfloat16)
    grad_probs = jnp.einsum(
        "qhd,khd->hqk", grad_mixed_heads, value_heads, preferred_element_type=jnp.float32
    )
    row_inner = jnp.sum(prob_full * grad_probs, axis=2, keepdims=True)
    grad_scores = (prob_full * (grad_probs - row_inner)).astype(jnp.bfloat16)
    grad_query_blocks = jnp.einsum(
        "hqk,khd->qhd", grad_scores, key_heads, preferred_element_type=jnp.float32
    )
    grad_keys_part = jnp.einsum(
        "hqk,qhd->khd", grad_scores, query_heads, preferred_element_type=jnp.float32
    )
    grad_values_part = jnp.einsum(
        "hqk,qhd->khd", prob_low, grad_mixed_heads, preferred_element_type=jnp.float32
    )
    grad_table = skew_grad(grad_scores, onehot, block_rows, slot_span)
    grad_keys_own, grad_values_own = (
        lax.psum_scatter(
            grad_keys_part.astype(jnp.bfloat16), "group", scatter_dimension=0, tiled=True
        ).astype(jnp.float32),
        lax.psum_scatter(
            grad_values_part.astype(jnp.bfloat16), "group", scatter_dimension=0, tiled=True
        ).astype(jnp.float32),
    )
    grad_query_low = grad_query_blocks.reshape(local_rows, width).astype(jnp.bfloat16)
    grad_keys_low = grad_keys_own.reshape(local_rows, width).astype(jnp.bfloat16)
    grad_values_low = grad_values_own.reshape(local_rows, width).astype(jnp.bfloat16)
    grad_w_query = product_tn(normed_low, grad_query_low)
    grad_w_keys = product_tn(normed_low, grad_keys_low)
    grad_w_values = product_tn(normed_low, grad_values_low)
    grad_normed = (
        product_nt(grad_query_low, w_query)
        + product_nt(grad_keys_low, w_keys)
        + product_nt(grad_values_low, w_values)
    )
    grad_from_attn, grad_gain_attn = attn_norm_pull(grad_normed)
    grad_tokens = grad_hidden + grad_from_attn
    members = [
        grad_w_query,
        grad_w_keys,
        grad_w_values,
        grad_w_output,
        grad_w_gate,
        grad_w_up,
        grad_w_down,
        grad_gain_attn,
        grad_gain_ffn,
        grad_table,
    ]
    shard_rows = master.shape[0]
    grid = Grid(lax.axis_size("dp"))
    count = grid.devices
    stride, window = shard_rows - 1, shard_rows - 1 + count
    place = lax.axis_index("dp") * group_size + lax.axis_index("group")
    tail = jnp.concatenate([member.reshape(-1) for member in members[7:]])
    tail = jnp.pad(tail, (0, count * 128 - tail.shape[0])).reshape(count, 128)
    tail = lax.psum(tail, ("dp", "group"))
    flat = jnp.concatenate([member.astype(bf16).reshape(-1, 128) for member in members[:7]])
    flat = jnp.pad(flat, ((0, count), (0, 0)))
    summed = scatter_rows(flat, grid, 0, grid.planes, stride, window, 1)
    summed = jnp.where(
        (place == count - 1) & (jnp.arange(window) >= stride)[:, None],
        jnp.pad(tail, ((stride, 0), (0, 0))),
        summed,
    )
    grad_shard = lax.dynamic_slice_in_dim(summed, place, shard_rows, 0)
    moment_one_new, moment_two_new, master_new = adam_step(
        grad_shard, moment_one, moment_two, master
    )
    states = (moment_one, moment_two, master)
    ends = jnp.stack([state[shard_rows - count :] for state in states])
    ring = [(one, (one + 1) % count) for one in range(count)]
    before = lax.ppermute(ends, ("dp", "group"), ring)
    last = lax.psum(jnp.where(place == count - 1, ends, 0.0), ("dp", "group"))
    wide = [
        lax.dynamic_slice_in_dim(jnp.concatenate([before[k], states[k]]), count - place, stride, 0)
        for k in range(3)
    ]
    fresh = adam_step(summed[:stride], *wide)[2].astype(bf16)
    fresh_tail = adam_step(tail, *last)[2].astype(bf16)
    fresh_copy = gather_rows(fresh, fresh_tail, grid, stride, 2)
    return (
        layer_out,
        grad_tokens,
        grad_shard,
        moment_one_new,
        moment_two_new,
        master_new,
        fresh_copy,
    )


def solution(mesh):
    return jax.shard_map(
        per_device,
        mesh=mesh,
        in_specs=(
            P(("dp", "group"), None),
            P("dp"),
            P(("dp", "group"), None),
            P(),
            P(),
            P(),
            P(),
            P(),
            P(),
            P(),
            P(),
            P(),
            P(),
            P(("dp", "group"), None),
            P(("dp", "group"), None),
            P(("dp", "group"), None),
        ),
        out_specs=(
            P(("dp", "group"), None),
            P(("dp", "group"), None),
            P(("dp", "group"), None),
            P(("dp", "group"), None),
            P(("dp", "group"), None),
            P(("dp", "group"), None),
            P(),
        ),
        check_vma=False,
    )
```

```python
import functools
import jax
import jax.numpy as jnp
from jax import lax
from jax.experimental import pallas as pl
from jax.experimental.pallas import tpu as pltpu
from jax.sharding import PartitionSpec as P

MESH = pl.DeviceIdType.MESH
bf16, f32 = jnp.bfloat16, jnp.float32
NN = (((1,), (0,)), ((), ()))
NT = (((1,), (1,)), ((), ()))
TN = (((0,), (0,)), ((), ()))
root_half = 0.7978845608028654


class Grid:
    def __init__(self, dp):
        half = dp // 2
        self.X = 1
        while self.X * self.X * 4 <= half:
            self.X *= 2
        self.planes = half // self.X
        self.devices = dp * 2
        self.swap = self.X == 2

    def here(self):
        return Grid(self.devices // 2).place()

    def place(self):
        dp = lax.axis_index("dp")
        self.core = lax.rem(dp, 2)
        self.x = lax.rem(lax.div(dp, 2), self.X)
        self.plane = lax.div(dp, 2 * self.X)
        self.y = lax.axis_index("group")
        self.flip = self.core if self.swap else 0
        if self.swap:
            self.a = jnp.where(self.core == 0, self.x, self.y)
            self.b = jnp.where(self.core == 0, self.y, self.x)
        else:
            self.a, self.b = self.x, self.y
        return self

    def xy(self, a, b):
        if not self.swap:
            return a, b
        return jnp.where(self.core == 0, a, b), jnp.where(self.core == 0, b, a)

    def device(self, plane=None, a=None, b=None, core=None):
        plane = self.plane if plane is None else plane
        a = self.a if a is None else a
        b = self.b if b is None else b
        x, y = self.xy(a, b)
        core = self.core if core is None else core
        return ((plane * self.X + x) * 2 + core, y)

    def index(self, plane, x, core, y):
        return ((plane * self.X + x) * 2 + core) * 2 + y

    def partners(self):
        found = [self.device(core=1 - self.core), self.device(b=1 - self.b)]
        found += [self.device(a=lax.rem(self.a + d, self.X)) for d in range(1, self.X)]
        found += [self.device(plane=lax.rem(self.plane + d, self.planes)) for d in range(1, self.planes)]
        return found


def enter(partners):
    barrier = pltpu.get_barrier_semaphore()
    for one in partners:
        pl.semaphore_signal(barrier, inc=1, device_id=one, device_id_type=MESH)
    pl.semaphore_wait(barrier, len(partners))


def add_rows(out, terms, rows, block):
    @pl.loop(0, rows // block)
    def _(step):
        part = pl.ds(pl.multiple_of(step * block, block), block)
        total = terms[0][part, :].astype(f32)
        for term in terms[1:]:
            total = total + term[part, :].astype(f32)
        out[part, :] = total.astype(out.dtype)


def block_of(rows):
    for tiles in range(12, 0, -1):
        if rows % (16 * tiles) == 0:
            return 16 * tiles


class Scatter:
    def __init__(self, grid, first, count, stride, window, base=0, pairs=0):
        self.g, self.first, self.count, self.stride, self.window = grid, first, count, stride, window
        self.base, self.pairs = base, pairs

    def scratch(self):
        g, n, w = self.g, self.count, self.window
        dma = pltpu.SemaphoreType.DMA
        return [
            pltpu.VMEM((n, g.X, 2, w, 128), bf16),
            pltpu.VMEM((n, g.X, 2, w, 128), bf16),
            pltpu.VMEM((n, g.X - 1, 2, w, 128), bf16),
            pltpu.VMEM((n, w, 128), bf16),
            dma((n, g.X, 2)), dma((n, g.X, 2)), dma((n, g.X, 2)),
            dma((n, g.X - 1, 2)), dma((n, g.X - 1, 2)),
            dma((n,)), dma((n,)), dma((n,)), dma((g.planes - 1,)),
        ]

    def shared(self):
        return [
            pltpu.VMEM((self.g.planes - 1, self.window, 128), bf16),
            pltpu.VMEM((self.window, 128), bf16),
        ]

    def bind(self, flat, out, scratch, shared):
        self.r4, self.kept = shared
        (self.own, self.r1, self.r2, self.r3, self.lsem, self.s1, self.q1, self.s2,
         self.q2, self.s3, self.q3, self.s4, self.q4) = scratch
        self.flat, self.out, self.g = flat, out, self.g.here()

    def plane_of(self, k):
        return self.first + lax.rem(self.g.plane + 1 + k, self.count)

    def copies0(self, k):
        g = self.g
        q = self.plane_of(k)
        for x in range(g.X):
            for y in range(2):
                there = pl.multiple_of(self.stride * g.index(q, x, 1 - g.core, y) - self.base, 16)
                here = pl.multiple_of(self.stride * g.index(q, x, g.core, y) - self.base, 16)
                yield (
                    pltpu.make_async_remote_copy(
                        self.flat.at[pl.ds(there, self.window), :], self.r1.at[k, x, y],
                        self.s1.at[k, x, y], self.q1.at[k, x, y],
                        device_id=g.device(core=1 - g.core), device_id_type=MESH),
                    pltpu.make_async_copy(
                        self.flat.at[pl.ds(here, self.window), :], self.own.at[k, x, y], self.lsem.at[k, x, y]),
                    x, y)

    def copies1(self, k):
        g = self.g
        for d in range(1, g.X):
            a = lax.rem(g.a + d, g.X)
            for b in range(2):
                x, y = g.xy(a, b)
                yield pltpu.make_async_remote_copy(
                    self.own.at[k, x, y], self.r2.at[k, d - 1, b], self.s2.at[k, d - 1, b], self.q2.at[k, d - 1, b],
                    device_id=g.device(a=a), device_id_type=MESH)

    def copy2(self, k):
        g = self.g
        x, y = g.xy(g.a, 1 - g.b)
        return pltpu.make_async_remote_copy(
            self.own.at[k, x, y], self.r3.at[k], self.s3.at[k], self.q3.at[k],
            device_id=g.device(b=1 - g.b), device_id_type=MESH)

    def copy3(self, k):
        g = self.g
        q = self.plane_of(k)
        slot = lax.rem(g.plane - q + g.planes, g.planes) - 1
        slot = jnp.maximum(slot, 0)
        return pltpu.make_async_remote_copy(
            self.own.at[k, g.x, g.y], self.r4.at[slot], self.s4.at[k], self.q4.at[slot],
            device_id=g.device(plane=q), device_id_type=MESH)

    def step(self, stage, k):
        g = self.g
        block = block_of(self.window)
        if stage == 0:
            for far, near, x, y in self.copies0(k):
                far.start()
                near.start()
        elif stage == 1:
            for far, near, x, y in self.copies0(k):
                near.wait()
                far.wait()
                add_rows(self.own.at[k, x, y], [self.own.at[k, x, y], self.r1.at[k, x, y]], self.window, block)
            for copy in self.copies1(k):
                copy.start()
        elif stage == 2:
            for copy in self.copies1(k):
                copy.wait()
            for b in range(2):
                x, y = g.xy(g.a, b)
                mine = self.own.at[k, x, y]
                add_rows(mine, [mine] + [self.r2.at[k, d, b] for d in range(g.X - 1)], self.window, block)
            self.copy2(k).start()
        elif stage == 3:
            self.copy2(k).wait()
            mine = self.own.at[k, g.x, g.y]
            q = self.plane_of(k)
            add_rows(mine, [mine, self.r3.at[k]], self.window, block)

            @pl.when(q != g.plane)
            def _():
                self.copy3(k).start()

            @pl.when(q == g.plane)
            def _():
                add_rows(self.kept, [mine], self.window, block)

    def finish(self):
        g = self.g
        for k in range(self.count):
            @pl.when(self.plane_of(k) != g.plane)
            def _():
                self.copy3(k).wait_send()

        inside = jnp.logical_and(g.plane >= self.first, g.plane < self.first + self.count)

        @pl.when(inside)
        def _():
            for d in range(g.planes - 1):
                pltpu.make_async_remote_copy(
                    self.kept, self.r4.at[d], self.s4.at[0], self.q4.at[d],
                    device_id=g.device(plane=lax.rem(g.plane + 1 + d, g.planes)), device_id_type=MESH).wait_recv()
            add_rows(self.out, [self.kept] + [self.r4.at[d] for d in range(g.planes - 1)], self.window,
                     block_of(self.window))

    def order(self):
        found = [(1, k) for k in range(self.count)]
        for t in range(self.count + 1):
            found += [(stage, k) for stage, k in ((2, t), (3, t - 1)) if 0 <= k < self.count]
        return found

    def all(self):
        for k in range(self.count):
            self.step(0, k)
        for stage, k in self.order():
            self.step(stage, k)
        self.finish()


def gather_kernel(grid, stride, fresh, tail, out, lsem, tsem, s0, q0, s1, q1, s2, q2, s3, q3):
    g = grid.here()
    enter(g.partners())
    X, planes = g.X, g.planes

    def rows(q, x, core, y):
        return out.at[pl.ds(pl.multiple_of(stride * g.index(q, x, core, y), 16), stride), :]

    mine = rows(g.plane, g.x, g.core, g.y)
    first = pltpu.make_async_copy(fresh, mine, lsem)
    first.start()
    rest = pltpu.make_async_copy(tail, out.at[pl.ds(stride * g.devices, g.devices), :], tsem)
    rest.start()

    def send0(d):
        return pltpu.make_async_remote_copy(
            fresh, mine, s0.at[d - 1], q0.at[d - 1],
            device_id=g.device(plane=lax.rem(g.plane + d, planes)), device_id_type=MESH)

    def plane_of(k):
        return lax.rem(g.plane - k + planes, planes)

    def send1(k):
        part = rows(plane_of(k), g.x, g.core, g.y)
        return pltpu.make_async_remote_copy(
            part, part, s1.at[k], q1.at[k], device_id=g.device(b=1 - g.b), device_id_type=MESH)

    def send2(k):
        for d in range(1, X):
            for b in range(2):
                x, y = g.xy(g.a, b)
                part = rows(plane_of(k), x, g.core, y)
                yield pltpu.make_async_remote_copy(
                    part, part, s2.at[k, d - 1, b], q2.at[k, d - 1, b],
                    device_id=g.device(a=lax.rem(g.a + d, X)), device_id_type=MESH)

    def send3(k):
        for x in range(X):
            for y in range(2):
                part = rows(plane_of(k), x, g.core, y)
                yield pltpu.make_async_remote_copy(
                    part, part, s3.at[k, x, y], q3.at[k, x, y],
                    device_id=g.device(core=1 - g.core), device_id_type=MESH)

    for d in range(1, planes):
        send0(d).start()
    first.wait()
    for t in range(planes + 2):
        if t < planes:
            if t > 0:
                send0(t).wait_recv()
            send1(t).start()
        k = t - 1
        if 0 <= k < planes:
            send1(k).wait_recv()
            for copy in send2(k):
                copy.start()
        k = t - 2
        if 0 <= k < planes:
            for copy in send2(k):
                copy.wait_recv()
            for copy in send3(k):
                copy.start()
    for k in range(planes):
        for copy in send3(k):
            copy.wait_recv()
    for d in range(1, planes):
        send0(d).wait_send()
    for k in range(planes):
        send1(k).wait_send()
        for copy in send2(k):
            copy.wait_send()
        for copy in send3(k):
            copy.wait_send()
    rest.wait()


def gather_rows(fresh, tail, grid, stride, collective_id):
    dma = pltpu.SemaphoreType.DMA
    n, X = grid.planes, grid.X
    total = (stride + 1) * grid.devices
    return pl.pallas_call(
        functools.partial(gather_kernel, grid, stride),
        out_shape=jax.ShapeDtypeStruct((total, 128), bf16),
        in_specs=[pl.BlockSpec(memory_space=pl.ANY)] * 2,
        out_specs=pl.BlockSpec(memory_space=pl.ANY),
        scratch_shapes=[dma, dma, dma((n - 1,)), dma((n - 1,)), dma((n,)), dma((n,)),
                        dma((n, X - 1, 2)), dma((n, X - 1, 2)), dma((n, X, 2)), dma((n, X, 2))],
        compiler_params=pltpu.CompilerParams(collective_id=collective_id, has_side_effects=True),
    )(fresh, tail)


def lane_mask(rows, head):
    lane = lax.broadcasted_iota(jnp.int32, (rows, 128), 1)
    return (lane < 64) if head == 0 else (lane >= 64)


far_steps = (8, 12, 16, 23, 32, 46, 64, 91)


def bucket_index(offset):
    distance = jnp.abs(offset)
    passed = sum((distance >= one).astype(jnp.int32) for one in far_steps)
    inside = jnp.where(distance < 8, distance, 7 + passed)
    return inside + 16 * (offset > 0).astype(jnp.int32)


def near_rows(table, rows, span, first_row):
    spans = rows // 128
    blocks = span // 128 + spans
    offset = (
        128 * (jnp.arange(blocks, dtype=jnp.int32)[:, None] - (spans - 1))
        - jnp.arange(128, dtype=jnp.int32)[None, :] - first_row)
    onehot = (bucket_index(offset)[None] == jnp.arange(table.shape[0], dtype=jnp.int32)[:, None, None])
    return jnp.sum(jnp.where(onehot[:, None], table.astype(f32)[:, :, None, None], 0.0), axis=0)


def dot_of(left, right, dims):
    return lax.dot_general(left, right, dims, preferred_element_type=f32)


def flatten_into(value, wide, out, first):
    rows, columns = value.shape
    parts = columns // 128
    for part in range(parts):
        wide[pl.ds(part, rows, stride=parts), :] = value[:, 128 * part : 128 * part + 128]
    size = rows * parts
    out[pl.ds(first, size), :] = wide[pl.ds(0, size), :].astype(bf16)


def ffn_kernel(steps, tall, bases, length, x_ref, mixed_ref, cot_ref, gain_ref, wo_ref, wg_ref, wu_ref, wd_ref,
               out_ref, ghid_ref, gmix_ref, ggain_ref, flat_ref,
               flat, wide, hidden, nf, nft, gout, gate_low, up_low, out_sum, gnf_sum, sems):
    step = pl.program_id(0)
    rows, width = x_ref.shape
    chunk = wg_ref.shape[1]
    o_base, g_base, u_base, d_base, end = bases
    parts = wg_ref.shape[0] // 128

    @pl.when(step == 0)
    def _():
        place = lax.broadcasted_iota(jnp.int32, (rows, width), 0) + lax.rem(lax.axis_index("dp"), 2) * rows
        cot = cot_ref[...]
        gout[...] = jnp.where(place < length[0:1, 0:1], cot, jnp.zeros_like(cot))
        total = x_ref[...].astype(f32) + dot_of(mixed_ref[...], wo_ref[...], NN)
        hidden[...] = total
        scale = lax.rsqrt(jnp.mean(total * total, axis=1, keepdims=True) + 1e-06)
        normed = (total * scale * gain_ref[...].astype(f32)).astype(bf16)
        nf[...] = normed
        nft[...] = normed.T
        out_sum[...] = total
        gnf_sum[...] = jnp.zeros_like(gnf_sum)
        flat[pl.ds(end, flat.shape[0] - end), :] = jnp.zeros((flat.shape[0] - end, 128), bf16)

    @pl.when(step < steps)
    def _():
        gate = dot_of(nf[...], wg_ref[...], NN)
        up = dot_of(nf[...], wu_ref[...], NN)
        ginner = dot_of(gout[...], wd_ref[...], NT)
        square = gate * gate
        th = jnp.tanh(root_half * (gate + 0.044715 * gate * square))
        half = 0.5 * (1.0 + th)
        act = gate * half
        slope = half + 0.5 * gate * (1.0 - th * th) * (root_half * (1.0 + 3 * 0.044715 * square))
        inner = (act * up).astype(bf16)
        ggate = (ginner * up * slope).astype(bf16)
        gup = (ginner * act).astype(bf16)
        gate_low[:, pl.ds(pl.multiple_of(step * chunk, chunk), chunk)] = ggate
        up_low[:, pl.ds(pl.multiple_of(step * chunk, chunk), chunk)] = gup
        out_sum[...] += dot_of(inner, wd_ref[...], NN)
        gnf_sum[...] += dot_of(ggate, wg_ref[...], NT) + dot_of(gup, wu_ref[...], NT)
        size = chunk * (width // 128)
        flatten_into(dot_of(inner, gout[...], TN), wide, flat, pl.multiple_of(d_base + step * size, 16))
        part = pl.ds(pl.multiple_of(d_base + step * size, 16), size)
        pltpu.make_async_copy(flat.at[part, :], flat_ref.at[part, :], sems.at[step]).start()

    @pl.when(step == steps - 1)
    def _():
        out_ref[...] = out_sum[...].astype(bf16)
        total = hidden[...]
        scale = lax.rsqrt(jnp.mean(total * total, axis=1, keepdims=True) + 1e-06)
        unit = total * scale
        grad = gnf_sum[...]
        ggain_ref[...] = jnp.sum(grad * unit, axis=0, keepdims=True)
        c2 = grad * gain_ref[...].astype(f32)
        ghid = gout[...].astype(f32) + scale * (c2 - unit * jnp.mean(c2 * unit, axis=1, keepdims=True))
        ghid_ref[...] = ghid
        branch = ghid.astype(bf16)
        gmix_ref[...] = dot_of(branch, wo_ref[...], NT).astype(bf16)
        size = width * width // 128
        flatten_into(dot_of(mixed_ref[...], branch, TN), wide, flat, o_base)
        part = pl.ds(o_base, size)
        pltpu.make_async_copy(flat.at[part, :], flat_ref.at[part, :], sems.at[steps]).start()

    turns = width // tall
    for k, (low, base) in enumerate(((gate_low, g_base), (up_low, u_base))):
        @pl.when(jnp.logical_and(step >= steps + k * turns, step < steps + (k + 1) * turns))
        def _():
            turn = step - steps - k * turns
            columns = low.shape[1]
            size = tall * columns // 128
            value = dot_of(nft[pl.ds(pl.multiple_of(turn * tall, tall), tall), :], low[...], NN)
            first = pl.multiple_of(base + turn * size, 16)
            flatten_into(value, wide, flat, first)
            pltpu.make_async_copy(flat.at[pl.ds(first, size), :], flat_ref.at[pl.ds(first, size), :], sems.at[step + 1]).start()

    @pl.when(step == steps + 2 * turns - 1)
    def _():
        rest = flat.shape[0] - end
        last = pltpu.make_async_copy(flat.at[pl.ds(end, rest), :], flat_ref.at[pl.ds(end, rest), :], sems.at[steps + 2 * turns + 1])
        last.start()
        for s in range(steps):
            size = chunk * (width // 128)
            part = pl.ds(d_base + s * size, size)
            pltpu.make_async_copy(flat.at[part, :], flat_ref.at[part, :], sems.at[s]).wait()
        part = pl.ds(o_base, width * width // 128)
        pltpu.make_async_copy(flat.at[part, :], flat_ref.at[part, :], sems.at[steps]).wait()
        for k, base in enumerate((g_base, u_base)):
            size = tall * gate_low.shape[1] // 128
            for turn in range(turns):
                part = pl.ds(base + turn * size, size)
                pltpu.make_async_copy(flat.at[part, :], flat_ref.at[part, :], sems.at[steps + k * turns + turn + 1]).wait()
        last.wait()


def ffn(length, x, mixed, cot, gain, wo, wg, wu, wd, pad_rows):
    rows, width = x.shape
    deep = wg.shape[1]
    chunk, tall = 256, 256
    steps = deep // chunk
    turns = width // tall
    square, oblong = width * width // 128, width * deep // 128
    bases = (0, square, square + oblong, square + 2 * oblong, square + 3 * oblong)
    total = bases[4] + pad_rows
    whole = lambda shape: pl.BlockSpec(shape, lambda s: (0, 0))
    at = lambda s: jnp.minimum(s, steps - 1)
    return pl.pallas_call(
        functools.partial(ffn_kernel, steps, tall, bases),
        grid=(steps + 2 * turns,),
        in_specs=[whole(length.shape), whole((rows, width)), whole((rows, width)), whole((rows, width)), whole((1, width)),
                  whole((width, width)),
                  pl.BlockSpec((width, chunk), lambda s: (0, at(s))),
                  pl.BlockSpec((width, chunk), lambda s: (0, at(s))),
                  pl.BlockSpec((chunk, width), lambda s: (at(s), 0))],
        out_specs=[whole((rows, width)), whole((rows, width)), whole((rows, width)), whole((1, width)),
                   pl.BlockSpec(memory_space=pl.ANY)],
        out_shape=[jax.ShapeDtypeStruct((rows, width), bf16), jax.ShapeDtypeStruct((rows, width), f32),
                   jax.ShapeDtypeStruct((rows, width), bf16), jax.ShapeDtypeStruct((1, width), f32),
                   jax.ShapeDtypeStruct((total, 128), bf16)],
        scratch_shapes=[
            pltpu.VMEM((total, 128), bf16), pltpu.VMEM((max(tall * deep, square * 128) // 128, 128), f32),
            pltpu.VMEM((rows, width), f32), pltpu.VMEM((rows, width), bf16), pltpu.VMEM((width, rows), bf16),
            pltpu.VMEM((rows, width), bf16), pltpu.VMEM((rows, deep), bf16), pltpu.VMEM((rows, deep), bf16),
            pltpu.VMEM((rows, width), f32), pltpu.VMEM((rows, width), f32),
            pltpu.SemaphoreType.DMA((steps + 2 * turns + 2,))],
        compiler_params=pltpu.CompilerParams(vmem_limit_bytes=56 << 20),
    )(length, x, mixed, cot, gain, wo, wg, wu, wd)


def near_toeplitz(y_ref, head, b):
    near = jnp.concatenate([y_ref[head, b : b + 1, :], y_ref[head, b + 1 : b + 2, :]], axis=1)
    return pltpu.roll(jnp.broadcast_to(near, (128, 256)), 0, 1, stride=1, stride_axis=0)[:, :128]


def front_kernel(grid, chunk, tok_ref, cot_ref, len_ref, gain_ref, wq_ref, wk_ref, wv_ref, y_ref,
                 x_out, cot_out, len_out, normed_out, q_out, k_out, v_out, mixed_out, prob_ref,
                 xs, cs, ls, keys, values, bias, score, sems, s_kv, r_kv):
    g = grid.here()
    pair = pl.program_id(0)
    rows, width = tok_ref.shape
    span = keys.shape[0]
    spans = rows // 128
    blocks = span // 128 + spans - 1
    mate = g.device(core=1 - g.core)
    dp = lax.axis_index("dp")
    twin = (dp - g.core + g.y, g.core)
    moved = g.core != g.y
    first = pl.multiple_of(g.core * rows, rows)

    def move(k, begin):
        src, dst = ((tok_ref, xs), (cot_ref, cs))[k]

        @pl.when(moved)
        def _():
            far = pltpu.make_async_remote_copy(
                src, dst, sems.at[2 * k], sems.at[2 * k + 1], device_id=twin, device_id_type=MESH)
            far.start() if begin else far.wait()

        @pl.when(jnp.logical_not(moved))
        def _():
            near = pltpu.make_async_copy(src, dst, sems.at[2 * k + 1])
            near.start() if begin else near.wait()

    lens_copy = lambda: pltpu.make_async_remote_copy(len_ref, ls, sems.at[4], sems.at[5], device_id=mate, device_id_type=MESH)

    def swaps():
        part = pl.ds(first, rows)
        for k, buf in enumerate((keys, values)):
            yield pltpu.make_async_remote_copy(buf.at[part, :], buf.at[part, :], s_kv.at[k], r_kv.at[k], device_id=mate, device_id_type=MESH)

    @pl.when(pair == 0)
    def _():
        barrier = pltpu.get_barrier_semaphore()
        pl.semaphore_signal(barrier, inc=1, device_id=mate, device_id_type=MESH)

        @pl.when(moved)
        def _():
            pl.semaphore_signal(barrier, inc=1, device_id=twin, device_id_type=MESH)

        pl.semaphore_wait(barrier, jnp.where(moved, 2, 1))
        move(0, True)
        move(1, True)
        lens = lens_copy()
        lens.start()
        move(0, False)
        wide = xs[...].astype(f32)
        normed = (wide * lax.rsqrt(jnp.mean(wide * wide, axis=1, keepdims=True) + 1e-06)
                  * gain_ref[...].astype(f32)).astype(bf16)
        x_out[...] = xs[...]
        normed_out[...] = normed
        keys[pl.ds(first, rows), :] = dot_of(normed, wk_ref[...], NN).astype(bf16)
        values[pl.ds(first, rows), :] = dot_of(normed, wv_ref[...], NN).astype(bf16)
        for copy in swaps():
            copy.start()
        q_out[...] = dot_of(normed, wq_ref[...], NN).astype(bf16)
        lens.wait()
        len_out[...] = jnp.where(moved, ls[...], len_ref[...])
        for copy in swaps():
            copy.wait()

    lanes = pl.ds(pl.multiple_of(128 * pair, 128), 128)
    live = len_out[0:1, 0:1]
    for head in range(2):
        for b in range(blocks):
            bias[head, pl.ds(128 * b, 128), :] = near_toeplitz(y_ref, head, b)
    halves = []
    for head in range(2):
        query = q_out[:, lanes]
        query = jnp.where(lane_mask(rows, head), query, jnp.zeros_like(query))
        top = jnp.full((1, rows), -jnp.inf, f32)
        for c in range(span // chunk):
            part = pl.ds(chunk * c, chunk)
            raw = dot_of(keys[part, lanes], query, NT)
            added = jnp.concatenate(
                [bias[head, pl.ds(128 * (spans - 1 - s) + chunk * c, chunk), :] for s in range(spans)], axis=1)
            place = lax.broadcasted_iota(jnp.int32, (chunk, rows), 0) + chunk * c
            raw = jnp.where(place < live, raw + added, -jnp.inf)
            score[head, part, :] = raw
            top = jnp.maximum(top, jnp.max(raw, axis=0, keepdims=True))
        total = jnp.zeros((1, rows), f32)
        for c in range(span // chunk):
            part = pl.ds(chunk * c, chunk)
            grown = jnp.exp(score[head, part, :] - top)
            score[head, part, :] = grown
            total = total + jnp.sum(grown, axis=0, keepdims=True)
        inverse = 1.0 / total
        for c in range(span // chunk):
            part = pl.ds(chunk * c, chunk)
            prob_ref[head, part, :] = (score[head, part, :] * inverse).astype(bf16)
        halves.append(dot_of(values[:, lanes], prob_ref[head], TN))
    both = jnp.concatenate([halves[0][:64], halves[1][64:]], axis=0)
    mixed_out[:, lanes] = both.T.astype(bf16)

    @pl.when(pair == pl.num_programs(0) - 1)
    def _():
        k_out[...] = keys[...]
        v_out[...] = values[...]
        move(1, False)
        cot_out[...] = cs[...]


def once(shape):
    return pl.BlockSpec(shape, lambda s: (0,) * len(shape), pipeline_mode=pl.Buffered(1))


def front(grid, tokens, cot, lens, gain, wq, wk, wv, near, collective_id):
    rows, width = tokens.shape
    span, pairs, blocks = 2 * rows, width // 128, near.shape[1]
    row_shape, key_shape = (rows, width), (span, width)
    dma = pltpu.SemaphoreType.DMA
    return pl.pallas_call(
        functools.partial(front_kernel, grid, 256),
        grid=(pairs,),
        in_specs=[once(row_shape), once(row_shape), once(lens.shape), once((1, width)),
                  once((width, width)), once((width, width)), once((width, width)),
                  pl.BlockSpec((2, blocks, 128), lambda p: (p, 0, 0))],
        out_specs=[once(row_shape), once(row_shape), once(lens.shape), once(row_shape), once(row_shape),
                   once(key_shape), once(key_shape), once(row_shape),
                   pl.BlockSpec((2, span, rows), lambda p: (p, 0, 0))],
        out_shape=[jax.ShapeDtypeStruct(s, t) for s, t in (
            (row_shape, bf16), (row_shape, bf16), (lens.shape, jnp.int32), (row_shape, bf16), (row_shape, bf16),
            (key_shape, bf16), (key_shape, bf16), (row_shape, bf16), ((2 * pairs, span, rows), bf16))],
        scratch_shapes=[pltpu.VMEM(row_shape, bf16), pltpu.VMEM(row_shape, bf16), pltpu.VMEM(lens.shape, jnp.int32),
                        pltpu.VMEM(key_shape, bf16), pltpu.VMEM(key_shape, bf16),
                        pltpu.VMEM((2, 128 * (blocks - 1), 128), f32), pltpu.VMEM((2, span, rows), f32),
                        dma((6,)), dma((2,)), dma((2,))],
        compiler_params=pltpu.CompilerParams(collective_id=collective_id, has_side_effects=True, vmem_limit_bytes=56 << 20),
    )(tokens, cot, lens, gain, wq, wk, wv, near)


class TailSum:
    def __init__(self, grid, rows):
        self.g, self.rows = grid, rows
        self.sizes = (2, grid.X, 2, grid.planes)

    def scratch(self):
        dma = pltpu.SemaphoreType.DMA
        return [pltpu.VMEM((size, self.rows, 128), f32) for size in self.sizes] + [
            dma((sum(self.sizes),)), dma((sum(self.sizes),))]

    def bind(self, scratch):
        self.bufs, self.send, self.recv = scratch[:4], scratch[4], scratch[5]
        self.g = g = self.g.here()
        self.places = (g.core, g.a, g.b, g.plane)

    def mate(self, axis, place):
        g = self.g
        return (g.device(core=place), g.device(a=place), g.device(b=place), g.device(plane=place))[axis]

    def mine(self, axis):
        return self.bufs[axis].at[self.places[axis]]

    def copies(self, axis):
        base = sum(self.sizes[:axis])
        for d in range(1, self.sizes[axis]):
            there = lax.rem(self.places[axis] + d, self.sizes[axis])
            buf = self.bufs[axis]
            yield pltpu.make_async_remote_copy(
                buf.at[self.places[axis]], buf.at[self.places[axis]], self.send.at[base + d], self.recv.at[base + d],
                device_id=self.mate(axis, there), device_id_type=MESH)

    def start(self, axis):
        for copy in self.copies(axis):
            copy.start()

    def done(self, axis):
        for copy in self.copies(axis):
            copy.wait_send()
        base = sum(self.sizes[:axis])
        for d in range(1, self.sizes[axis]):
            behind = lax.rem(self.places[axis] - d + self.sizes[axis], self.sizes[axis])
            buf = self.bufs[axis]
            pltpu.make_async_remote_copy(
                buf.at[behind], buf.at[behind], self.send.at[base + d], self.recv.at[base + d],
                device_id=self.mate(axis, behind), device_id_type=MESH).wait_recv()
        total = self.bufs[axis][0]
        for k in range(1, self.sizes[axis]):
            total = total + self.bufs[axis][k]
        return total


def adam_step(grads, moment_one, moment_two, master):
    moment_one_new = 0.9 * moment_one + 0.1 * grads
    moment_two_new = 0.999 * moment_two + 0.001 * grads * grads
    first_hat = moment_one_new / (1.0 - 0.9**10)
    second_hat = moment_two_new / (1.0 - 0.999**10)
    master_new = master - 0.01 * (first_hat / (jnp.sqrt(second_hat) + 1e-08) + 0.1 * master)
    return moment_one_new, moment_two_new, master_new


def dot_exact(left, right):
    return lax.dot_general(left, right, NN, precision=lax.Precision.HIGHEST, preferred_element_type=f32)


def diagonals(block):
    row = lax.broadcasted_iota(jnp.int32, (128, 128), 0)
    lane = lax.broadcasted_iota(jnp.int32, (128, 128), 1)
    turned = dot_exact(block, (row + lane == 127).astype(f32))
    wide = jnp.concatenate([turned, jnp.zeros_like(turned)], axis=1)
    return jnp.sum(pltpu.roll(wide, 0, 1, stride=1, stride_axis=0), axis=0, keepdims=True)


def table_rows(diag, far, heads, buckets):
    tall = diag.shape[1]
    lane = lax.broadcasted_iota(jnp.int32, (tall, 128), 1)
    sums = jnp.where(lane == buckets // 2 - 1, jnp.sum(far[0], axis=1, keepdims=True), 0.0)
    sums = sums + jnp.where(lane == buckets - 1, jnp.sum(far[1], axis=1, keepdims=True), 0.0)
    for n in range(3):
        offset = lax.broadcasted_iota(jnp.int32, (256, 128), 0) - 127 + 128 * (n - 1)
        onehot = bucket_index(offset) == lax.broadcasted_iota(jnp.int32, (256, 128), 1)
        sums = sums + dot_exact(diag[n], onehot.astype(f32))
    found = []
    for t in range(heads * buckets // 128):
        place = lax.broadcasted_iota(jnp.int32, (128, 128), 1) + 128 * t
        bucket = lax.broadcasted_iota(jnp.int32, (128, 128), 0)
        spread = jnp.logical_and(place >= heads * bucket, place < heads * bucket + heads)
        wide = dot_exact(sums, spread.astype(f32))
        place = lax.broadcasted_iota(jnp.int32, (tall, 128), 1) + 128 * t
        head = place - heads * ((place * (65536 // heads + 1)) >> 16)
        mine = head == lax.broadcasted_iota(jnp.int32, (tall, 128), 0)
        found.append(jnp.sum(jnp.where(mine, wide, 0.0), axis=0, keepdims=True))
    return found


def back_kernel(grid, chunk, early, late, ends, heads, buckets, *refs):
    (q_ref, k_ref, v_ref, gm_ref, mixed_ref, prob_ref, normed_ref, x_ref, ghid_ref, gain_ref, wq_ref, wk_ref, wv_ref,
     lo_ref, ggain_ref, m1_ref, m2_ref, ma_ref, flat_ref,
     lo_out, gtok_out, gshard_out, m1_out, m2_out, ma_out, fresh_out, ftail_out) = refs[:27]
    rest = refs[27:]
    taken = []
    for job in (early, late, ends):
        size = len(job.scratch())
        taken.append(rest[:size])
        rest = rest[size:]
    shared, rest = rest[:2], rest[2:]
    (slope, gq, gk, gv, rk, rv, flat, wide, diag, far, lo_in, gt_in, halo, halo_in, summed, renewed,
     lsem, s_kv, r_kv, s_turn, r_turn) = rest
    g = grid.here()
    step = pl.program_id(0)
    rows, width = normed_ref.shape
    keys = k_ref.shape[0]
    spans = rows // 128
    blocks = keys // 128 + spans - 1
    pairs = pl.num_programs(0) - 1
    first = spans - 1 + g.core * spans
    mate = g.device(core=1 - g.core)
    dp = lax.axis_index("dp")
    twin = (dp - g.core + g.y, g.core)
    moved = g.core != g.y
    count = grid.devices
    place = dp * 2 + g.y
    after = lax.rem(place + 1, count)
    nextdoor = (lax.div(after, 2), lax.rem(after, 2))
    before = lax.rem(place + count - 1, count)
    prior = (lax.div(before, 2), lax.rem(before, 2))
    shard = ma_ref.shape[0]
    stride, window = early.stride, early.window
    early.bind(flat_ref, summed.at[pl.ds(count, window), :], taken[0], shared)
    late.bind(flat, summed.at[pl.ds(count, window), :], taken[1], shared)
    ends.bind(taken[2])
    order = early.order()
    square = width * width // 128
    over = flat.shape[0] - 3 * square
    edge = lambda: pltpu.make_async_copy(flat_ref.at[pl.ds(0, over), :], flat.at[pl.ds(3 * square, over), :], lsem.at[0])
    lo_copy = lambda: pltpu.make_async_remote_copy(
        lo_ref, lo_in, s_turn.at[0], r_turn.at[0], device_id=twin, device_id_type=MESH)
    ghid_copy = lambda: pltpu.make_async_copy(ghid_ref, gtok_out, lsem.at[1])
    lo_stay = lambda: pltpu.make_async_copy(lo_ref, lo_in, r_turn.at[0])
    gt_copy = lambda: pltpu.make_async_remote_copy(
        gq, gt_in, s_turn.at[1], r_turn.at[1], device_id=twin, device_id_type=MESH)
    halo_copy = lambda: pltpu.make_async_remote_copy(
        halo, halo_in, s_turn.at[2], r_turn.at[2], device_id=nextdoor, device_id_type=MESH)

    def square_grad(right, base):
        half = width // 2
        for k in range(2):
            flatten_into(dot_of(normed_ref[:, half * k : half * k + half], right, TN), wide, flat, base + k * square // 2)

    @pl.when(step == 0)
    def _():
        barrier = pltpu.get_barrier_semaphore()
        partners = g.partners() + [prior, nextdoor]
        for one in partners:
            pl.semaphore_signal(barrier, inc=1, device_id=one, device_id_type=MESH)

        @pl.when(moved)
        def _():
            pl.semaphore_signal(barrier, inc=1, device_id=twin, device_id_type=MESH)

        pl.semaphore_wait(barrier, len(partners) + jnp.where(moved, 1, 0))
        edge().start()
        ghid_copy().start()
        for k in range(early.count):
            early.step(0, k)
        for k, state in enumerate((m1_ref, m2_ref, ma_ref)):
            halo[k] = state[pl.ds(shard - count, count), :]
        halo_copy().start()

        @pl.when(moved)
        def _():
            lo_copy().start()

        @pl.when(jnp.logical_not(moved))
        def _():
            lo_stay().start()

    for n, (stage, k) in enumerate(order):
        if n + 1 < late.pairs:
            @pl.when(step == n + 1)
            def _():
                early.step(stage, k)

    @pl.when(step < pairs)
    def _():
        inner = (gm_ref[...].astype(f32) * mixed_ref[...].astype(f32)).T
        parts = ([], [], [])
        for head in range(2):
            row_inner = jnp.sum(inner[64 * head : 64 * head + 64], axis=0, keepdims=True)
            grown = gm_ref[...]
            grown = jnp.where(lane_mask(rows, head), grown, jnp.zeros_like(grown))
            for c in range(keys // chunk):
                part = pl.ds(chunk * c, chunk)
                back = dot_of(v_ref[part, :], grown, NT)
                slope[head, part, :] = (prob_ref[head, part, :].astype(f32) * (back - row_inner)).astype(bf16)
            parts[0].append(dot_of(k_ref[...], slope[head], TN))
            parts[1].append(dot_of(slope[head], q_ref[...], NN))
            parts[2].append(dot_of(prob_ref[head], gm_ref[...], NN))
            low = jnp.zeros((8, 128), f32)
            high = jnp.zeros((8, 128), f32)
            mids = [jnp.zeros((128, 128), f32) for _ in range(3)]
            for b in range(blocks):
                total = None
                for s in range(spans):
                    j = b - (spans - 1) + s
                    if 0 <= j < keys // 128:
                        term = slope[head, pl.ds(128 * j, 128), pl.ds(128 * s, 128)].astype(f32)
                        total = term if total is None else total + term
                wide[pl.ds(128 * b, 128), :] = total
                folded = total.reshape(16, 8, 128).sum(axis=0)
                low = low + jnp.where(b < first - 1, folded, 0.0)
                high = high + jnp.where(b > first + 1, folded, 0.0)
            line = pl.ds(2 * step + head, 1)
            for n in range(3):
                near = wide[pl.ds(pl.multiple_of(128 * (first - 1 + n), 128), 128), :]
                diag[n, line, :] = diagonals(near)
            far[0, line, :] = jnp.sum(low, axis=0, keepdims=True)
            far[1, line, :] = jnp.sum(high, axis=0, keepdims=True)
        lanes = pl.ds(pl.multiple_of(128 * step, 128), 128)
        gq[:, lanes] = jnp.concatenate([parts[0][0][:64], parts[0][1][64:]], axis=0).T.astype(bf16)
        mask = lane_mask(keys, 0)
        gk[:, lanes] = jnp.where(mask, parts[1][0], parts[1][1]).astype(bf16)
        gv[:, lanes] = jnp.where(mask, parts[2][0], parts[2][1]).astype(bf16)

    @pl.when(step == pairs)
    def _():
        mine = pl.ds(pl.multiple_of(g.core * rows, rows), rows)
        other = pl.ds(pl.multiple_of((1 - g.core) * rows, rows), rows)
        copies = [pltpu.make_async_remote_copy(a.at[other, :], b, s_kv.at[k], r_kv.at[k], device_id=mate, device_id_type=MESH)
                  for k, (a, b) in enumerate(((gk, rk), (gv, rv)))]
        for copy in copies:
            copy.start()
        square_grad(gq[...], 0)
        total = dot_of(gq[...], wq_ref[...], NT)
        for k, (a, b, w) in enumerate(((gk, rk, wk_ref), (gv, rv, wv_ref))):
            copies[k].wait()
            low = (a[mine, :].astype(f32) + b[...].astype(f32)).astype(bf16)
            b[...] = low
            square_grad(low, (k + 1) * square)
            total = total + dot_of(low, w[...], NT)
        edge().wait()
        for k in range(late.count):
            late.step(0, k)
        x = x_ref[...].astype(f32)
        scale = lax.rsqrt(jnp.mean(x * x, axis=1, keepdims=True) + 1e-06)
        unit = x * scale
        gain_row = jnp.sum(total * unit, axis=0, keepdims=True)
        c1 = total * gain_ref[...].astype(f32)
        ghid_copy().wait()
        gtok = gtok_out[...] + scale * (c1 - unit * jnp.mean(c1 * unit, axis=1, keepdims=True))
        gtok_out[...] = gtok

        @pl.when(moved)
        def _():
            gq[...] = gtok.astype(bf16)
            gt_copy().start()

        tail = ends.mine(0)
        tail[...] = jnp.zeros(tail.shape, f32)
        for r in range(width // 128):
            tail[r : r + 1, :] = gain_row[:, 128 * r : 128 * r + 128]
            tail[width // 128 + r : width // 128 + r + 1, :] = ggain_ref[:, 128 * r : 128 * r + 128]
        for r, line in enumerate(table_rows(diag, far, heads, buckets)):
            tail[2 * width // 128 + r : 2 * width // 128 + r + 1, :] = line
        for k in range(3):
            tail[16 + k * count : 16 + (k + 1) * count, :] = jnp.where(place == count - 1, halo[k], 0.0)
        ends.start(0)

        left = [(early, stage, k) for n, (stage, k) in enumerate(order) if n + 1 >= late.pairs]
        left += [(late, stage, k) for stage, k in late.order()]
        for n, (job, stage, k) in enumerate(left):
            job.step(stage, k)
            if n < 3:
                found = ends.done(n)
                ends.mine(n + 1)[...] = found
                ends.start(n + 1)
        found = ends.done(3)
        summed[pl.ds(0, count), :] = jnp.zeros((count, 128), f32)
        early.finish()
        late.finish()

        @pl.when(place == count - 1)
        def _():
            summed[pl.ds(count + stride, count), :] = jnp.zeros((count, 128), f32)
            summed[pl.ds(count + stride, 16), :] = found[:16]

        grads = jnp.concatenate([found[:16], jnp.zeros((count - 16, 128), f32)], axis=0)
        last = [found[16 + k * count : 16 + (k + 1) * count] for k in range(3)]
        ftail_out[...] = adam_step(grads, *last)[2].astype(bf16)
        halo_copy().wait()
        renewed[pl.ds(0, count), :] = adam_step(summed[pl.ds(place, count), :], *[halo_in[k] for k in range(3)])[2]
        for start in range(0, shard, 216):
            size = min(216, shard - start)
            part = pl.ds(start, size)
            grads = summed[pl.ds(place + count + start, size), :]
            one, two, new = adam_step(grads, m1_ref[part, :], m2_ref[part, :], ma_ref[part, :])
            gshard_out[part, :] = grads
            m1_out[part, :] = one
            m2_out[part, :] = two
            ma_out[part, :] = new
            renewed[pl.ds(count + start, size), :] = new
        for start in range(0, stride, stride // 8):
            fresh_out[pl.ds(start, stride // 8), :] = renewed[pl.ds(start + count - place, stride // 8), :].astype(bf16)

        @pl.when(moved)
        def _():
            lo_copy().wait()
            gt_copy().wait()
            gtok_out[...] = gt_in[...].astype(f32)

        @pl.when(jnp.logical_not(moved))
        def _():
            lo_stay().wait()

        lo_out[...] = lo_in[...]


def back(grid, heads, buckets, query, keys_all, values_all, grad_mixed, mixed, prob, normed, x, grad_hidden, gain,
         wq, wk, wv, layer_out, ggain, moment_one, moment_two, master, flat, collective_id):
    rows, width = query.shape
    span = keys_all.shape[0]
    pairs = width // 128
    shard = master.shape[0]
    count = grid.devices
    stride, window = shard - 1, shard - 1 + count
    cut = grid.planes // 4
    late_rows = 3 * width * width // 128
    early = Scatter(grid, cut, grid.planes - cut, stride, window, late_rows, pairs)
    late = Scatter(grid, 0, cut, stride, window, 0, pairs)
    ends = TailSum(grid, 16 + 3 * count)
    at = lambda s: jnp.minimum(s, pairs - 1)
    tall = lambda n: pl.BlockSpec((n, 128), lambda s: (0, at(s)))
    dma = pltpu.SemaphoreType.DMA
    state = (shard, 128)
    return pl.pallas_call(
        functools.partial(back_kernel, grid, 256, early, late, ends, heads, buckets),
        grid=(pairs + 1,),
        in_specs=[tall(rows), tall(span), tall(span), tall(rows), tall(rows),
                  pl.BlockSpec((2, span, rows), lambda s: (at(s), 0, 0)),
                  once((rows, width)), once((rows, width)), pl.BlockSpec(memory_space=pl.ANY), once((1, width)),
                  once((width, width)), once((width, width)), once((width, width)),
                  pl.BlockSpec(memory_space=pl.ANY), once((1, width)), once(state), once(state), once(state),
                  pl.BlockSpec(memory_space=pl.ANY)],
        out_specs=[once((rows, width)), once((rows, width)), once(state), once(state), once(state), once(state),
                   once((stride, 128)), once((count, 128))],
        out_shape=[jax.ShapeDtypeStruct(s, t) for s, t in (
            ((rows, width), bf16), ((rows, width), f32), (state, f32), (state, f32), (state, f32), (state, f32),
            ((stride, 128), bf16), ((count, 128), bf16))],
        scratch_shapes=early.scratch() + late.scratch() + ends.scratch() + early.shared() + [
            pltpu.VMEM((2, span, rows), bf16), pltpu.VMEM((rows, width), bf16),
            pltpu.VMEM((span, width), bf16), pltpu.VMEM((span, width), bf16),
            pltpu.VMEM((rows, width), bf16), pltpu.VMEM((rows, width), bf16),
            pltpu.VMEM((late_rows + count, 128), bf16), pltpu.VMEM((late_rows // 6, 128), f32),
            pltpu.VMEM((3, 16, 256), f32), pltpu.VMEM((2, 16, 128), f32),
            pltpu.VMEM((rows, width), bf16), pltpu.VMEM((rows, width), bf16),
            pltpu.VMEM((3, count, 128), f32), pltpu.VMEM((3, count, 128), f32),
            pltpu.VMEM((count + window, 128), f32), pltpu.VMEM((count + shard + 7, 128), f32),
            dma((2,)), dma((2,)), dma((2,)), dma((3,)), dma((3,))],
        compiler_params=pltpu.CompilerParams(collective_id=collective_id, has_side_effects=True, vmem_limit_bytes=62 << 20),
    )(query, keys_all, values_all, grad_mixed, mixed, prob, normed, x, grad_hidden, gain, wq, wk, wv, layer_out, ggain,
      moment_one, moment_two, master, flat)


def per_device(tokens, lengths, cotangent, w_query, w_keys, w_values, w_output, w_gate, w_up, w_down,
               gain_attn, gain_ffn, bias_table, master, moment_one, moment_two):
    rows, width = tokens.shape
    grid = Grid(lax.axis_size("dp")).here()
    span = rows * lax.axis_size("group")
    count = grid.devices
    first_row = grid.core * rows
    near = near_rows(bias_table, rows, span, first_row)
    lens = jnp.broadcast_to(lengths.reshape(1, 1), (8, 128))
    gain_one, gain_two = gain_attn.reshape(1, width), gain_ffn.reshape(1, width)
    x, cot, lens, normed, query, keys_all, values_all, mixed, prob = front(
        grid, tokens, cotangent, lens, gain_one, w_query, w_keys, w_values, near, 1)
    layer_out, grad_hidden, grad_mixed, grad_gain_ffn, flat = ffn(
        lens, x, mixed, cot, gain_two, w_output, w_gate, w_up, w_down, count)
    layer_out, grad_tokens, grad_shard, moment_one_new, moment_two_new, master_new, fresh, fresh_tail = back(
        grid, bias_table.shape[1], bias_table.shape[0], query, keys_all, values_all, grad_mixed, mixed, prob, normed, x,
        grad_hidden, gain_one, w_query, w_keys, w_values, layer_out, grad_gain_ffn, moment_one, moment_two, master, flat, 2)
    fresh_copy = gather_rows(fresh, fresh_tail, grid, master.shape[0] - 1, 3)
    return (layer_out, grad_tokens, grad_shard, moment_one_new, moment_two_new, master_new, fresh_copy)


def solution(mesh):
    both = P(("dp", "group"), None)
    return jax.shard_map(
        per_device,
        mesh=mesh,
        in_specs=(both, P("dp"), both) + (P(),) * 10 + (both,) * 3,
        out_specs=(both,) * 6 + (P(),),
        check_vma=False,
    )
```

```python
import functools
import jax
import jax.numpy as jnp
from jax import lax
from jax.experimental import pallas as pl
from jax.experimental.pallas import tpu as pltpu
from jax.sharding import PartitionSpec as P

MESH = pl.DeviceIdType.MESH
bf16, f32 = jnp.bfloat16, jnp.float32
NN = (((1,), (0,)), ((), ()))
NT = (((1,), (1,)), ((), ()))
TN = (((0,), (0,)), ((), ()))
root_half = 0.7978845608028654


class Grid:
    def __init__(self, dp):
        half = dp // 2
        self.X = 1
        while self.X * self.X * 4 <= half:
            self.X *= 2
        self.planes = half // self.X
        self.devices = dp * 2
        self.swap = self.X == 2

    def here(self):
        return Grid(self.devices // 2).place()

    def place(self):
        dp = lax.axis_index("dp")
        self.core = lax.rem(dp, 2)
        self.x = lax.rem(lax.div(dp, 2), self.X)
        self.plane = lax.div(dp, 2 * self.X)
        self.y = lax.axis_index("group")
        self.flip = self.core if self.swap else 0
        if self.swap:
            self.a = jnp.where(self.core == 0, self.x, self.y)
            self.b = jnp.where(self.core == 0, self.y, self.x)
        else:
            self.a, self.b = self.x, self.y
        return self

    def xy(self, a, b):
        if not self.swap:
            return a, b
        return jnp.where(self.core == 0, a, b), jnp.where(self.core == 0, b, a)

    def device(self, plane=None, a=None, b=None, core=None):
        plane = self.plane if plane is None else plane
        a = self.a if a is None else a
        b = self.b if b is None else b
        x, y = self.xy(a, b)
        core = self.core if core is None else core
        return ((plane * self.X + x) * 2 + core, y)

    def index(self, plane, x, core, y):
        return ((plane * self.X + x) * 2 + core) * 2 + y

    def partners(self):
        found = [self.device(core=1 - self.core), self.device(b=1 - self.b)]
        found += [self.device(a=lax.rem(self.a + d, self.X)) for d in range(1, self.X)]
        found += [self.device(plane=lax.rem(self.plane + d, self.planes)) for d in range(1, self.planes)]
        return found


def enter(partners):
    barrier = pltpu.get_barrier_semaphore()
    for one in partners:
        pl.semaphore_signal(barrier, inc=1, device_id=one, device_id_type=MESH)
    pl.semaphore_wait(barrier, len(partners))


def add_rows(out, terms, rows, block):
    @pl.loop(0, rows // block)
    def _(step):
        part = pl.ds(pl.multiple_of(step * block, block), block)
        total = terms[0][part, :].astype(f32)
        for term in terms[1:]:
            total = total + term[part, :].astype(f32)
        out[part, :] = total.astype(out.dtype)


def block_of(rows):
    for tiles in range(12, 0, -1):
        if rows % (16 * tiles) == 0:
            return 16 * tiles


class Scatter:
    def __init__(self, grid, first, planes, stride, window, base, tree):
        self.g, self.first, self.owners, self.stride, self.window = grid, first, planes, stride, window
        self.base, self.tree = base, tree
        self.parts = 2 if window % 32 == 0 else 1
        self.rows = window // self.parts
        self.count = planes * self.parts
        self.levels = grid.planes.bit_length() - 1
        self.ahead = 3

    def scratch(self):
        g, n, w = self.g, self.count, self.rows
        dma = pltpu.SemaphoreType.DMA
        lines = self.levels * self.owners if self.tree else g.planes - 1
        return [
            pltpu.VMEM((n, g.X, 2, w, 128), bf16),
            pltpu.VMEM((n, g.X, 2, w, 128), bf16),
            pltpu.VMEM((n, g.X - 1, 2, w, 128), bf16),
            pltpu.VMEM((n, w, 128), bf16),
            pltpu.VMEM((lines, self.parts, w, 128), bf16),
            dma((n, g.X, 2)), dma((n, g.X, 2)), dma((n, g.X, 2)),
            dma((n, g.X - 1, 2)), dma((n, g.X - 1, 2)),
            dma((n,)), dma((n,)), dma((n,)), dma((lines, self.parts)),
        ]

    def bind(self, flat, out, scratch):
        (self.own, self.r1, self.r2, self.r3, self.r4, self.lsem, self.s1, self.q1, self.s2,
         self.q2, self.s3, self.q3, self.s4, self.q4) = scratch
        self.flat, self.out, self.g = flat, out, self.g.here()

    def plane_of(self, k):
        n, j = self.owners, k // self.parts
        g = self.g
        return self.first + lax.rem(g.plane - self.first + n + 1 + j, n)

    def add(self, out, terms):
        add_rows(out, terms, self.rows, block_of(self.rows))

    def copies0(self, k):
        g = self.g
        q = self.plane_of(k)
        shift = k % self.parts * self.rows - self.base
        for x in range(g.X):
            for y in range(2):
                there = pl.multiple_of(self.stride * g.index(q, x, 1 - g.core, y) + shift, 16)
                here = pl.multiple_of(self.stride * g.index(q, x, g.core, y) + shift, 16)
                yield (
                    pltpu.make_async_remote_copy(
                        self.flat.at[pl.ds(there, self.rows), :], self.r1.at[k, x, y],
                        self.s1.at[k, x, y], self.q1.at[k, x, y],
                        device_id=g.device(core=1 - g.core), device_id_type=MESH),
                    pltpu.make_async_copy(
                        self.flat.at[pl.ds(here, self.rows), :], self.own.at[k, x, y], self.lsem.at[k, x, y]),
                    x, y)

    def copies1(self, k):
        g = self.g
        for d in range(1, g.X):
            a = lax.rem(g.a + d, g.X)
            for b in range(2):
                x, y = g.xy(a, b)
                yield pltpu.make_async_remote_copy(
                    self.own.at[k, x, y], self.r2.at[k, d - 1, b], self.s2.at[k, d - 1, b], self.q2.at[k, d - 1, b],
                    device_id=g.device(a=a), device_id_type=MESH)

    def copy2(self, k):
        g = self.g
        x, y = g.xy(g.a, 1 - g.b)
        return pltpu.make_async_remote_copy(
            self.own.at[k, x, y], self.r3.at[k], self.s3.at[k], self.q3.at[k],
            device_id=g.device(b=1 - g.b), device_id_type=MESH)

    def distance(self, k):
        return lax.rem(self.g.plane - self.plane_of(k) + self.g.planes, self.g.planes)

    def copy3(self, k, line, plane):
        g = self.g
        part = k % self.parts
        return pltpu.make_async_remote_copy(
            self.own.at[k, g.x, g.y], self.r4.at[line, part], self.s4.at[k], self.q4.at[line, part],
            device_id=g.device(plane=plane), device_id_type=MESH)

    def climb(self, k, level, wait):
        far = self.distance(k)
        line = level * self.owners + self.plane_of(k) - self.first

        @pl.when(lax.rem(far, 2 << level) == 1 << level)
        def _():
            copy = self.copy3(k, line, lax.rem(self.g.plane - (1 << level) + self.g.planes, self.g.planes))
            copy.wait_send() if wait else copy.start()

    def step(self, stage, k):
        g = self.g
        if stage == 0:
            for far, near, x, y in self.copies0(k):
                far.start()
                near.start()
        elif stage == 1:
            for far, near, x, y in self.copies0(k):
                near.wait()
                far.wait()
                self.add(self.own.at[k, x, y], [self.own.at[k, x, y], self.r1.at[k, x, y]])
            if k < self.ahead:
                for copy in self.copies1(k):
                    copy.start()
        elif stage == 2:
            for copy in self.copies1(k):
                copy.wait()
            if k + self.ahead < self.count:
                for copy in self.copies1(k + self.ahead):
                    copy.start()
            for b in (1 - g.b, g.b):
                x, y = g.xy(g.a, b)
                mine = self.own.at[k, x, y]
                self.add(mine, [mine] + [self.r2.at[k, d, b] for d in range(g.X - 1)])
                if b is not g.b:
                    self.copy2(k).start()
        elif stage == 3:
            self.copy2(k).wait()
            mine = self.own.at[k, g.x, g.y]
            self.add(mine, [mine, self.r3.at[k]])
            if self.tree:
                self.climb(k, 0, False)
            else:
                far = self.distance(k)

                @pl.when(far > 0)
                def _():
                    self.copy3(k, far - 1, self.plane_of(k)).start()
        else:
            level = stage - 4
            far = self.distance(k)
            mine = self.own.at[k, g.x, g.y]
            line = level * self.owners + self.plane_of(k) - self.first

            @pl.when(lax.rem(far, 2 << level) == 0)
            def _():
                self.copy3(k, line, self.plane_of(k)).wait_recv()
                self.add(mine, [mine, self.r4.at[line, k % self.parts]])

            if level + 1 < self.levels:
                self.climb(k, level + 1, False)

    def finish(self):
        g = self.g
        for k in range(self.count):
            if self.tree:
                for level in range(self.levels):
                    self.climb(k, level, True)
            else:
                @pl.when(self.distance(k) > 0)
                def _():
                    self.copy3(k, 0, self.plane_of(k)).wait_send()

    def collect(self):
        g = self.g
        for part in range(self.parts):
            k = (self.owners - 1) * self.parts + part
            terms = [self.own.at[k, g.x, g.y]]
            if not self.tree:
                for d in range(g.planes - 1):
                    self.copy3(k, d, lax.rem(g.plane + 1 + d, g.planes)).wait_recv()
                    terms.append(self.r4.at[d, part])
            self.add(self.out.at[pl.ds(part * self.rows, self.rows), :], terms)


class Gather:
    def __init__(self, grid, stride):
        self.g, self.stride = grid, stride
        self.parts = 2 if stride % 32 == 0 else 1
        self.rows = stride // self.parts
        self.count = grid.planes * self.parts

    def scratch(self):
        dma = pltpu.SemaphoreType.DMA
        n, X, planes, parts = self.count, self.g.X, self.g.planes, self.parts
        return [dma((parts,)), dma((2 * planes - 1, parts)), dma((planes, parts)), dma((n,)), dma((n,)),
                dma((n, X - 1, 2)), dma((n, X - 1, 2)), dma((n, X, 2)), dma((n, X, 2))]

    def bind(self, fresh, out, scratch):
        self.lsem, self.s0, self.q0, self.s1, self.q1, self.s2, self.q2, self.s3, self.q3 = scratch
        self.fresh, self.out, self.g = fresh, out, self.g.here()

    def plane_of(self, k):
        g = self.g
        j = k // self.parts
        if g.planes == 4:
            one = jnp.where(g.plane == 0, (0, 1, 2, 3)[j], (1, 2, 0, 3)[j])
            other = jnp.where(g.plane == 2, (2, 1, 3, 0)[j], (3, 2, 1, 0)[j])
            return jnp.where(g.plane < 2, one, other)
        up = g.planes - 1 - g.plane
        return jnp.where(j <= up, g.plane + j, g.plane - (j - up))

    def part(self, q, x, core, y, part):
        g = self.g
        start = self.stride * g.index(q, x, core, y) + part * self.rows
        return self.out.at[pl.ds(pl.multiple_of(start, 16), self.rows), :]

    def first(self, part):
        g = self.g
        return pltpu.make_async_copy(
            self.fresh.at[pl.ds(part * self.rows, self.rows), :], self.part(g.plane, g.x, g.core, g.y, part), self.lsem.at[part])

    def send0(self, part, way):
        g = self.g
        rows = self.part(g.plane, g.x, g.core, g.y, part)
        slot = way + g.planes - 1
        return pltpu.make_async_remote_copy(
            self.fresh.at[pl.ds(part * self.rows, self.rows), :], rows, self.s0.at[slot, part], self.q0.at[g.plane, part],
            device_id=g.device(plane=jnp.clip(g.plane + way, 0, g.planes - 1)), device_id_type=MESH)

    def came0(self, q, part):
        g = self.g
        rows = self.part(q, g.x, g.core, g.y, part)
        return pltpu.make_async_remote_copy(
            rows, rows, self.s0.at[0, part], self.q0.at[q, part], device_id=g.device(plane=q), device_id_type=MESH)

    def reach(self, far, wait):
        g = self.g
        for part in range(self.parts):
            for way in (-far, far):
                @pl.when(jnp.logical_and(g.plane + way >= 0, g.plane + way < g.planes))
                def _():
                    copy = self.send0(part, way)
                    copy.wait_send() if wait else copy.start()

    def send1(self, k):
        g = self.g
        rows = self.part(self.plane_of(k), g.x, g.core, g.y, k % self.parts)
        return pltpu.make_async_remote_copy(
            rows, rows, self.s1.at[k], self.q1.at[k], device_id=g.device(b=1 - g.b), device_id_type=MESH)

    def send2(self, k):
        g = self.g
        for d in range(1, g.X):
            for b in range(2):
                x, y = g.xy(g.a, (g.b, 1 - g.b)[b])
                rows = self.part(self.plane_of(k), x, g.core, y, k % self.parts)
                yield pltpu.make_async_remote_copy(
                    rows, rows, self.s2.at[k, d - 1, b], self.q2.at[k, d - 1, b],
                    device_id=g.device(a=lax.rem(g.a + d, g.X)), device_id_type=MESH)

    def send3(self, k):
        g = self.g
        for x in range(g.X):
            for y in range(2):
                rows = self.part(self.plane_of(k), x, g.core, y, k % self.parts)
                yield pltpu.make_async_remote_copy(
                    rows, rows, self.s3.at[k, x, y], self.q3.at[k, x, y],
                    device_id=g.device(core=1 - g.core), device_id_type=MESH)

    def begin(self):
        for far in range(1, self.g.planes):
            self.reach(far, False)
        for part in range(self.parts):
            self.first(part).start()

    def step(self, stage, k):
        g = self.g
        q, part = self.plane_of(k), k % self.parts
        if stage == 0:
            @pl.when(q == g.plane)
            def _():
                self.first(part).wait()

            @pl.when(q != g.plane)
            def _():
                self.came0(q, part).wait_recv()

            self.send1(k).start()
            for n, copy in enumerate(self.send2(k)):
                if n % 2 == 0:
                    copy.start()
        elif stage == 1:
            self.send1(k).wait_recv()
            for n, copy in enumerate(self.send2(k)):
                if n % 2 == 1:
                    copy.start()
        else:
            for copy in self.send2(k):
                copy.wait_recv()
            for copy in self.send3(k):
                copy.start()

    def finish(self):
        for far in range(1, self.g.planes):
            self.reach(far, True)
        for k in range(self.count):
            self.send1(k).wait_send()
            for copy in self.send2(k):
                copy.wait_send()
            for copy in self.send3(k):
                copy.wait()


def lane_mask(rows, head):
    lane = lax.broadcasted_iota(jnp.int32, (rows, 128), 1)
    return (lane < 64) if head == 0 else (lane >= 64)


far_steps = (8, 12, 16, 23, 32, 46, 64, 91)


def bucket_index(offset):
    distance = jnp.abs(offset)
    passed = sum((distance >= one).astype(jnp.int32) for one in far_steps)
    inside = jnp.where(distance < 8, distance, 7 + passed)
    return inside + 16 * (offset > 0).astype(jnp.int32)


def near_rows(table, rows, span, first_row):
    spans = rows // 128
    blocks = span // 128 + spans
    offset = (
        128 * (jnp.arange(blocks, dtype=jnp.int32)[:, None] - (spans - 1))
        - jnp.arange(128, dtype=jnp.int32)[None, :] - first_row)
    onehot = (bucket_index(offset)[None] == jnp.arange(table.shape[0], dtype=jnp.int32)[:, None, None])
    return jnp.sum(jnp.where(onehot[:, None], table.astype(f32)[:, :, None, None], 0.0), axis=0)


def dot_of(left, right, dims):
    return lax.dot_general(left, right, dims, preferred_element_type=f32)


def flatten_into(value, wide, out, first):
    rows, columns = value.shape
    parts = columns // 128
    for part in range(parts):
        wide[pl.ds(part, rows, stride=parts), :] = value[:, 128 * part : 128 * part + 128]
    size = rows * parts
    out[pl.ds(first, size), :] = wide[pl.ds(0, size), :].astype(bf16)


def ffn_kernel(steps, tall, bases, length, x_ref, mixed_ref, cot_ref, gain_ref, wo_ref, wg_ref, wu_ref, wd_ref,
               out_ref, ghid_ref, gmix_ref, ggain_ref, flat_ref,
               flat, wide, hidden, nf, nft, gout, gate_low, up_low, out_sum, gnf_sum, sems, lo_send, lo_in, turn):
    step = pl.program_id(0)
    rows, width = x_ref.shape
    chunk = wg_ref.shape[1]
    o_base, g_base, u_base, d_base, end = bases
    dp, y = lax.axis_index("dp"), lax.axis_index("group")
    core = lax.rem(dp, 2)
    twin = (dp - core + y, core)
    moved = core != y
    lo_copy = lambda: pltpu.make_async_remote_copy(
        lo_send, lo_in, turn.at[0], turn.at[1], device_id=twin, device_id_type=MESH)

    @pl.when(jnp.logical_and(step == 0, moved))
    def _():
        barrier = pltpu.get_barrier_semaphore()
        pl.semaphore_signal(barrier, inc=1, device_id=twin, device_id_type=MESH)

    @pl.when(jnp.logical_and(step == steps - 1, moved))
    def _():
        pl.semaphore_wait(pltpu.get_barrier_semaphore(), 1)

    @pl.when(step == 0)
    def _():
        place = lax.broadcasted_iota(jnp.int32, (rows, width), 0) + lax.rem(lax.axis_index("dp"), 2) * rows
        cot = cot_ref[...]
        gout[...] = jnp.where(place < length[0:1, 0:1], cot, jnp.zeros_like(cot))
        total = x_ref[...].astype(f32) + dot_of(mixed_ref[...], wo_ref[...], NN)
        hidden[...] = total
        scale = lax.rsqrt(jnp.mean(total * total, axis=1, keepdims=True) + 1e-06)
        normed = (total * scale * gain_ref[...].astype(f32)).astype(bf16)
        nf[...] = normed
        nft[...] = normed.T
        out_sum[...] = total
        gnf_sum[...] = jnp.zeros_like(gnf_sum)
        flat[pl.ds(end, flat.shape[0] - end), :] = jnp.zeros((flat.shape[0] - end, 128), bf16)

    @pl.when(step < steps)
    def _():
        gate = dot_of(nf[...], wg_ref[...], NN)
        up = dot_of(nf[...], wu_ref[...], NN)
        ginner = dot_of(gout[...], wd_ref[...], NT)
        square = gate * gate
        th = jnp.tanh(root_half * (gate + 0.044715 * gate * square))
        half = 0.5 * (1.0 + th)
        act = gate * half
        slope = half + 0.5 * gate * (1.0 - th * th) * (root_half * (1.0 + 3 * 0.044715 * square))
        inner = (act * up).astype(bf16)
        ggate = (ginner * up * slope).astype(bf16)
        gup = (ginner * act).astype(bf16)
        gate_low[:, pl.ds(pl.multiple_of(step * chunk, chunk), chunk)] = ggate
        up_low[:, pl.ds(pl.multiple_of(step * chunk, chunk), chunk)] = gup
        out_sum[...] += dot_of(inner, wd_ref[...], NN)
        gnf_sum[...] += dot_of(ggate, wg_ref[...], NT) + dot_of(gup, wu_ref[...], NT)
        size = chunk * (width // 128)
        flatten_into(dot_of(inner, gout[...], TN), wide, flat, pl.multiple_of(d_base + step * size, 16))
        part = pl.ds(pl.multiple_of(d_base + step * size, 16), size)
        pltpu.make_async_copy(flat.at[part, :], flat_ref.at[part, :], sems.at[step]).start()

    @pl.when(step == steps - 1)
    def _():
        low = out_sum[...].astype(bf16)
        out_ref[...] = low

        @pl.when(moved)
        def _():
            lo_send[...] = low
            lo_copy().start()

        total = hidden[...]
        scale = lax.rsqrt(jnp.mean(total * total, axis=1, keepdims=True) + 1e-06)
        unit = total * scale
        grad = gnf_sum[...]
        ggain_ref[...] = jnp.sum(grad * unit, axis=0, keepdims=True)
        c2 = grad * gain_ref[...].astype(f32)
        ghid = gout[...].astype(f32) + scale * (c2 - unit * jnp.mean(c2 * unit, axis=1, keepdims=True))
        ghid_ref[...] = ghid
        branch = ghid.astype(bf16)
        gmix_ref[...] = dot_of(branch, wo_ref[...], NT).astype(bf16)
        size = width * width // 128
        flatten_into(dot_of(mixed_ref[...], branch, TN), wide, flat, o_base)
        part = pl.ds(o_base, size)
        pltpu.make_async_copy(flat.at[part, :], flat_ref.at[part, :], sems.at[steps]).start()

    turns = width // tall
    for k, (low, base) in enumerate(((gate_low, g_base), (up_low, u_base))):
        @pl.when(jnp.logical_and(step >= steps + k * turns, step < steps + (k + 1) * turns))
        def _():
            turn = step - steps - k * turns
            columns = low.shape[1]
            size = tall * columns // 128
            value = dot_of(nft[pl.ds(pl.multiple_of(turn * tall, tall), tall), :], low[...], NN)
            first = pl.multiple_of(base + turn * size, 16)
            flatten_into(value, wide, flat, first)
            pltpu.make_async_copy(flat.at[pl.ds(first, size), :], flat_ref.at[pl.ds(first, size), :], sems.at[step + 1]).start()

    @pl.when(step == steps + 2 * turns - 1)
    def _():
        rest = flat.shape[0] - end
        last = pltpu.make_async_copy(flat.at[pl.ds(end, rest), :], flat_ref.at[pl.ds(end, rest), :], sems.at[steps + 2 * turns + 1])
        last.start()
        for s in range(steps):
            size = chunk * (width // 128)
            part = pl.ds(d_base + s * size, size)
            pltpu.make_async_copy(flat.at[part, :], flat_ref.at[part, :], sems.at[s]).wait()
        part = pl.ds(o_base, width * width // 128)
        pltpu.make_async_copy(flat.at[part, :], flat_ref.at[part, :], sems.at[steps]).wait()
        for k, base in enumerate((g_base, u_base)):
            size = tall * gate_low.shape[1] // 128
            for turn in range(turns):
                part = pl.ds(base + turn * size, size)
                pltpu.make_async_copy(flat.at[part, :], flat_ref.at[part, :], sems.at[steps + k * turns + turn + 1]).wait()
        last.wait()

        @pl.when(moved)
        def _():
            lo_copy().wait()
            out_ref[...] = lo_in[...]


def ffn(length, x, mixed, cot, gain, wo, wg, wu, wd, pad_rows, collective_id):
    rows, width = x.shape
    deep = wg.shape[1]
    chunk, tall = 256, 256
    steps = deep // chunk
    turns = width // tall
    square, oblong = width * width // 128, width * deep // 128
    bases = (0, square, square + oblong, square + 2 * oblong, square + 3 * oblong)
    total = bases[4] + pad_rows
    whole = lambda shape: pl.BlockSpec(shape, lambda s: (0, 0))
    at = lambda s: jnp.minimum(s, steps - 1)
    return pl.pallas_call(
        functools.partial(ffn_kernel, steps, tall, bases),
        grid=(steps + 2 * turns,),
        in_specs=[whole(length.shape), whole((rows, width)), whole((rows, width)), whole((rows, width)), whole((1, width)),
                  whole((width, width)),
                  pl.BlockSpec((width, chunk), lambda s: (0, at(s))),
                  pl.BlockSpec((width, chunk), lambda s: (0, at(s))),
                  pl.BlockSpec((chunk, width), lambda s: (at(s), 0))],
        out_specs=[whole((rows, width)), whole((rows, width)), whole((rows, width)), whole((1, width)),
                   pl.BlockSpec(memory_space=pl.ANY)],
        out_shape=[jax.ShapeDtypeStruct((rows, width), bf16), jax.ShapeDtypeStruct((rows, width), f32),
                   jax.ShapeDtypeStruct((rows, width), bf16), jax.ShapeDtypeStruct((1, width), f32),
                   jax.ShapeDtypeStruct((total, 128), bf16)],
        scratch_shapes=[
            pltpu.VMEM((total, 128), bf16), pltpu.VMEM((max(tall * deep, square * 128) // 128, 128), f32),
            pltpu.VMEM((rows, width), f32), pltpu.VMEM((rows, width), bf16), pltpu.VMEM((width, rows), bf16),
            pltpu.VMEM((rows, width), bf16), pltpu.VMEM((rows, deep), bf16), pltpu.VMEM((rows, deep), bf16),
            pltpu.VMEM((rows, width), f32), pltpu.VMEM((rows, width), f32),
            pltpu.SemaphoreType.DMA((steps + 2 * turns + 2,)),
            pltpu.VMEM((rows, width), bf16), pltpu.VMEM((rows, width), bf16), pltpu.SemaphoreType.DMA((2,))],
        compiler_params=pltpu.CompilerParams(collective_id=collective_id, has_side_effects=True, vmem_limit_bytes=56 << 20),
    )(length, x, mixed, cot, gain, wo, wg, wu, wd)


def near_toeplitz(y_ref, head, b):
    near = jnp.concatenate([y_ref[head, b : b + 1, :], y_ref[head, b + 1 : b + 2, :]], axis=1)
    return pltpu.roll(jnp.broadcast_to(near, (128, 256)), 0, 1, stride=1, stride_axis=0)[:, :128]


def front_kernel(grid, chunk, tok_ref, cot_ref, len_ref, gain_ref, wq_ref, wk_ref, wv_ref, y_ref,
                 x_out, cot_out, len_out, normed_out, q_out, k_out, v_out, mixed_out, prob_ref,
                 xs, cs, ls, keys, values, bias, score, sems, s_kv, r_kv):
    g = grid.here()
    pair = pl.program_id(0)
    rows, width = tok_ref.shape
    span = keys.shape[0]
    spans = rows // 128
    blocks = span // 128 + spans - 1
    mate = g.device(core=1 - g.core)
    dp = lax.axis_index("dp")
    twin = (dp - g.core + g.y, g.core)
    moved = g.core != g.y
    first = pl.multiple_of(g.core * rows, rows)

    def move(k, begin):
        src, dst = ((tok_ref, xs), (cot_ref, cs))[k]

        @pl.when(moved)
        def _():
            far = pltpu.make_async_remote_copy(
                src, dst, sems.at[2 * k], sems.at[2 * k + 1], device_id=twin, device_id_type=MESH)
            far.start() if begin else far.wait()

        @pl.when(jnp.logical_not(moved))
        def _():
            near = pltpu.make_async_copy(src, dst, sems.at[2 * k + 1])
            near.start() if begin else near.wait()

    lens_copy = lambda: pltpu.make_async_remote_copy(len_ref, ls, sems.at[4], sems.at[5], device_id=mate, device_id_type=MESH)

    def swaps():
        part = pl.ds(first, rows)
        for k, buf in enumerate((keys, values)):
            yield pltpu.make_async_remote_copy(buf.at[part, :], buf.at[part, :], s_kv.at[k], r_kv.at[k], device_id=mate, device_id_type=MESH)

    @pl.when(pair == 0)
    def _():
        barrier = pltpu.get_barrier_semaphore()
        pl.semaphore_signal(barrier, inc=1, device_id=mate, device_id_type=MESH)

        @pl.when(moved)
        def _():
            pl.semaphore_signal(barrier, inc=1, device_id=twin, device_id_type=MESH)

        pl.semaphore_wait(barrier, jnp.where(moved, 2, 1))
        move(0, True)
        move(1, True)
        lens = lens_copy()
        lens.start()
        move(0, False)
        wide = xs[...].astype(f32)
        normed = (wide * lax.rsqrt(jnp.mean(wide * wide, axis=1, keepdims=True) + 1e-06)
                  * gain_ref[...].astype(f32)).astype(bf16)
        x_out[...] = xs[...]
        normed_out[...] = normed
        keys[pl.ds(first, rows), :] = dot_of(normed, wk_ref[...], NN).astype(bf16)
        values[pl.ds(first, rows), :] = dot_of(normed, wv_ref[...], NN).astype(bf16)
        for copy in swaps():
            copy.start()
        q_out[...] = dot_of(normed, wq_ref[...], NN).astype(bf16)
        lens.wait()
        len_out[...] = jnp.where(moved, ls[...], len_ref[...])
        for copy in swaps():
            copy.wait()

    lanes = pl.ds(pl.multiple_of(128 * pair, 128), 128)
    live = len_out[0:1, 0:1]
    for head in range(2):
        for b in range(blocks):
            bias[head, pl.ds(128 * b, 128), :] = near_toeplitz(y_ref, head, b)
    halves = []
    for head in range(2):
        query = q_out[:, lanes]
        query = jnp.where(lane_mask(rows, head), query, jnp.zeros_like(query))
        top = jnp.full((1, rows), -jnp.inf, f32)
        for c in range(span // chunk):
            part = pl.ds(chunk * c, chunk)
            raw = dot_of(keys[part, lanes], query, NT)
            added = jnp.concatenate(
                [bias[head, pl.ds(128 * (spans - 1 - s) + chunk * c, chunk), :] for s in range(spans)], axis=1)
            place = lax.broadcasted_iota(jnp.int32, (chunk, rows), 0) + chunk * c
            raw = jnp.where(place < live, raw + added, -jnp.inf)
            score[head, part, :] = raw
            top = jnp.maximum(top, jnp.max(raw, axis=0, keepdims=True))
        total = jnp.zeros((1, rows), f32)
        for c in range(span // chunk):
            part = pl.ds(chunk * c, chunk)
            grown = jnp.exp(score[head, part, :] - top)
            score[head, part, :] = grown
            total = total + jnp.sum(grown, axis=0, keepdims=True)
        inverse = 1.0 / total
        for c in range(span // chunk):
            part = pl.ds(chunk * c, chunk)
            prob_ref[head, part, :] = (score[head, part, :] * inverse).astype(bf16)
        halves.append(dot_of(values[:, lanes], prob_ref[head], TN))
    both = jnp.concatenate([halves[0][:64], halves[1][64:]], axis=0)
    mixed_out[:, lanes] = both.T.astype(bf16)

    @pl.when(pair == pl.num_programs(0) - 1)
    def _():
        k_out[...] = keys[...]
        v_out[...] = values[...]
        move(1, False)
        cot_out[...] = cs[...]


def once(shape):
    return pl.BlockSpec(shape, lambda s: (0,) * len(shape), pipeline_mode=pl.Buffered(1))


def front(grid, tokens, cot, lens, gain, wq, wk, wv, near, collective_id):
    rows, width = tokens.shape
    span, pairs, blocks = 2 * rows, width // 128, near.shape[1]
    row_shape, key_shape = (rows, width), (span, width)
    dma = pltpu.SemaphoreType.DMA
    return pl.pallas_call(
        functools.partial(front_kernel, grid, 256),
        grid=(pairs,),
        in_specs=[once(row_shape), once(row_shape), once(lens.shape), once((1, width)),
                  once((width, width)), once((width, width)), once((width, width)),
                  pl.BlockSpec((2, blocks, 128), lambda p: (p, 0, 0))],
        out_specs=[once(row_shape), once(row_shape), once(lens.shape), once(row_shape), once(row_shape),
                   once(key_shape), once(key_shape), once(row_shape),
                   pl.BlockSpec((2, span, rows), lambda p: (p, 0, 0))],
        out_shape=[jax.ShapeDtypeStruct(s, t) for s, t in (
            (row_shape, bf16), (row_shape, bf16), (lens.shape, jnp.int32), (row_shape, bf16), (row_shape, bf16),
            (key_shape, bf16), (key_shape, bf16), (row_shape, bf16), ((2 * pairs, span, rows), bf16))],
        scratch_shapes=[pltpu.VMEM(row_shape, bf16), pltpu.VMEM(row_shape, bf16), pltpu.VMEM(lens.shape, jnp.int32),
                        pltpu.VMEM(key_shape, bf16), pltpu.VMEM(key_shape, bf16),
                        pltpu.VMEM((2, 128 * (blocks - 1), 128), f32), pltpu.VMEM((2, span, rows), f32),
                        dma((6,)), dma((2,)), dma((2,))],
        compiler_params=pltpu.CompilerParams(collective_id=collective_id, has_side_effects=True, vmem_limit_bytes=56 << 20),
    )(tokens, cot, lens, gain, wq, wk, wv, near)


class TailSum:
    def __init__(self, grid, rows):
        self.g, self.rows = grid, rows
        self.sizes = (2, grid.X, 2, grid.planes)

    def scratch(self):
        dma = pltpu.SemaphoreType.DMA
        return [pltpu.VMEM((size, self.rows, 128), f32) for size in self.sizes] + [
            dma((sum(self.sizes),)), dma((sum(self.sizes),))]

    def bind(self, scratch):
        self.bufs, self.send, self.recv = scratch[:4], scratch[4], scratch[5]
        self.g = g = self.g.here()
        self.places = (g.core, g.a, g.b, g.plane)

    def mate(self, axis, place):
        g = self.g
        return (g.device(core=place), g.device(a=place), g.device(b=place), g.device(plane=place))[axis]

    def mine(self, axis):
        return self.bufs[axis].at[self.places[axis]]

    def copies(self, axis):
        base = sum(self.sizes[:axis])
        for d in range(1, self.sizes[axis]):
            there = lax.rem(self.places[axis] + d, self.sizes[axis])
            buf = self.bufs[axis]
            yield pltpu.make_async_remote_copy(
                buf.at[self.places[axis]], buf.at[self.places[axis]], self.send.at[base + d], self.recv.at[base + d],
                device_id=self.mate(axis, there), device_id_type=MESH)

    def start(self, axis):
        for copy in self.copies(axis):
            copy.start()

    def done(self, axis):
        for copy in self.copies(axis):
            copy.wait_send()
        base = sum(self.sizes[:axis])
        for d in range(1, self.sizes[axis]):
            behind = lax.rem(self.places[axis] - d + self.sizes[axis], self.sizes[axis])
            buf = self.bufs[axis]
            pltpu.make_async_remote_copy(
                buf.at[behind], buf.at[behind], self.send.at[base + d], self.recv.at[base + d],
                device_id=self.mate(axis, behind), device_id_type=MESH).wait_recv()
        total = self.bufs[axis][0]
        for k in range(1, self.sizes[axis]):
            total = total + self.bufs[axis][k]
        return total


def adam_step(grads, moment_one, moment_two, master):
    moment_one_new = 0.9 * moment_one + 0.1 * grads
    moment_two_new = 0.999 * moment_two + 0.001 * grads * grads
    first_hat = moment_one_new / (1.0 - 0.9**10)
    second_hat = moment_two_new / (1.0 - 0.999**10)
    master_new = master - 0.01 * (first_hat / (jnp.sqrt(second_hat) + 1e-08) + 0.1 * master)
    return moment_one_new, moment_two_new, master_new


def dot_exact(left, right):
    return lax.dot_general(left, right, NN, precision=lax.Precision.HIGHEST, preferred_element_type=f32)


def diagonals(block):
    row = lax.broadcasted_iota(jnp.int32, (128, 128), 0)
    lane = lax.broadcasted_iota(jnp.int32, (128, 128), 1)
    turned = dot_exact(block, (row + lane == 127).astype(f32))
    wide = jnp.concatenate([turned, jnp.zeros_like(turned)], axis=1)
    return jnp.sum(pltpu.roll(wide, 0, 1, stride=1, stride_axis=0), axis=0, keepdims=True)


def table_rows(diag, far, heads, buckets):
    tall = diag.shape[1]
    lane = lax.broadcasted_iota(jnp.int32, (tall, 128), 1)
    sums = jnp.where(lane == buckets // 2 - 1, jnp.sum(far[0], axis=1, keepdims=True), 0.0)
    sums = sums + jnp.where(lane == buckets - 1, jnp.sum(far[1], axis=1, keepdims=True), 0.0)
    for n in range(3):
        offset = lax.broadcasted_iota(jnp.int32, (256, 128), 0) - 127 + 128 * (n - 1)
        onehot = bucket_index(offset) == lax.broadcasted_iota(jnp.int32, (256, 128), 1)
        sums = sums + dot_exact(diag[n], onehot.astype(f32))
    found = []
    for t in range(heads * buckets // 128):
        place = lax.broadcasted_iota(jnp.int32, (128, 128), 1) + 128 * t
        bucket = lax.broadcasted_iota(jnp.int32, (128, 128), 0)
        spread = jnp.logical_and(place >= heads * bucket, place < heads * bucket + heads)
        wide = dot_exact(sums, spread.astype(f32))
        place = lax.broadcasted_iota(jnp.int32, (tall, 128), 1) + 128 * t
        head = place - heads * ((place * (65536 // heads + 1)) >> 16)
        mine = head == lax.broadcasted_iota(jnp.int32, (tall, 128), 0)
        found.append(jnp.sum(jnp.where(mine, wide, 0.0), axis=0, keepdims=True))
    return found


def back_kernel(grid, chunk, early, late, ends, spread, heads, buckets, *refs):
    (q_ref, k_ref, v_ref, gm_ref, mixed_ref, prob_ref, normed_ref, x_ref, ghid_ref, gain_ref, wq_ref, wk_ref, wv_ref,
     ggain_ref, m1_ref, m2_ref, ma_ref, flat_ref,
     gtok_out, gshard_out, m1_out, m2_out, ma_out, copy_out) = refs[:24]
    rest = refs[24:]
    taken = []
    for job in (early, late, ends, spread):
        size = len(job.scratch())
        taken.append(rest[:size])
        rest = rest[size:]
    (slope, gq, gk, gv, rk, rv, flat, wide, diag, far, gt_in, halo, halo_in, summed, renewed, fresh, ftail,
     lsem, s_kv, r_kv, s_turn, r_turn) = rest
    g = grid.here()
    step = pl.program_id(0)
    rows, width = normed_ref.shape
    keys = k_ref.shape[0]
    spans = rows // 128
    blocks = keys // 128 + spans - 1
    pairs = pl.num_programs(0) - 1
    first = spans - 1 + g.core * spans
    mate = g.device(core=1 - g.core)
    dp = lax.axis_index("dp")
    twin = (dp - g.core + g.y, g.core)
    moved = g.core != g.y
    count = grid.devices
    place = dp * 2 + g.y
    after = lax.rem(place + 1, count)
    nextdoor = (lax.div(after, 2), lax.rem(after, 2))
    before = lax.rem(place + count - 1, count)
    prior = (lax.div(before, 2), lax.rem(before, 2))
    shard = ma_ref.shape[0]
    stride, window = early.stride, early.window
    early.bind(flat_ref, summed.at[pl.ds(count, window), :], taken[0])
    late.bind(flat, summed.at[pl.ds(count, window), :], taken[1])
    ends.bind(taken[2])
    spread.bind(fresh, copy_out, taken[3])
    owner = g.plane >= early.first
    agenda = [(early, 1, k) for k in range(early.count)]
    split = early.count - 1
    jobs = [(early, k) for k in range(early.count)]
    jobs[split:split] = [(late, k) for k in range(late.count)]
    for n in range(len(jobs) + 1):
        agenda += [(job, stage, k) for stage, m in ((2, n), (3, n - 1)) if 0 <= m < len(jobs) for job, k in (jobs[m],)]
    square = width * width // 128
    over = flat.shape[0] - 3 * square
    edge = lambda: pltpu.make_async_copy(flat_ref.at[pl.ds(0, over), :], flat.at[pl.ds(3 * square, over), :], lsem.at[0])
    ghid_copy = lambda: pltpu.make_async_copy(ghid_ref, gtok_out, lsem.at[1])
    gt_copy = lambda: pltpu.make_async_remote_copy(
        gq, gt_in, s_turn.at[0], r_turn.at[0], device_id=twin, device_id_type=MESH)
    halo_copy = lambda: pltpu.make_async_remote_copy(
        halo, halo_in, s_turn.at[1], r_turn.at[1], device_id=nextdoor, device_id_type=MESH)

    def square_grad(right, base):
        third = width // 3
        for k in range(3):
            flatten_into(dot_of(normed_ref[:, third * k : third * k + third], right, TN), wide, flat, base + k * square // 3)

    @pl.when(step == 0)
    def _():
        barrier = pltpu.get_barrier_semaphore()
        partners = g.partners() + [prior, nextdoor]
        for one in partners:
            pl.semaphore_signal(barrier, inc=1, device_id=one, device_id_type=MESH)

        @pl.when(moved)
        def _():
            pl.semaphore_signal(barrier, inc=1, device_id=twin, device_id_type=MESH)

        pl.semaphore_wait(barrier, len(partners) + jnp.where(moved, 1, 0))
        edge().start()
        ghid_copy().start()
        for k in range(early.count):
            early.step(0, k)
        for k, state in enumerate((m1_ref, m2_ref, ma_ref)):
            halo[k] = state[pl.ds(shard - count, count), :]
        halo_copy().start()

    shares = [early.count * 2 // 6, early.count * 4 // 6, early.count * 5 // 6, early.count, early.count + 1]
    for n, (start, stop) in enumerate(zip([0] + shares[:-1], shares)):
        @pl.when(step == n + 1)
        def _():
            for job, stage, k in agenda[start:stop]:
                job.step(stage, k)

    pending = agenda[shares[-1] :]
    pending += [(late, 4 + level, k) for level in range(late.levels) for k in range(late.count)]

    def due(count, late_too=False):
        for _ in range(count):
            if pending and (late_too or pending[0][0] is early):
                job, stage, k = pending.pop(0)
                job.step(stage, k)

    @pl.when(step < pairs)
    def _():
        inner = (gm_ref[...].astype(f32) * mixed_ref[...].astype(f32)).T
        parts = ([], [], [])
        for head in range(2):
            row_inner = jnp.sum(inner[64 * head : 64 * head + 64], axis=0, keepdims=True)
            grown = gm_ref[...]
            grown = jnp.where(lane_mask(rows, head), grown, jnp.zeros_like(grown))
            for c in range(keys // chunk):
                part = pl.ds(chunk * c, chunk)
                back = dot_of(v_ref[part, :], grown, NT)
                slope[head, part, :] = (prob_ref[head, part, :].astype(f32) * (back - row_inner)).astype(bf16)
            parts[0].append(dot_of(k_ref[...], slope[head], TN))
            parts[1].append(dot_of(slope[head], q_ref[...], NN))
            parts[2].append(dot_of(prob_ref[head], gm_ref[...], NN))
            low = jnp.zeros((8, 128), f32)
            high = jnp.zeros((8, 128), f32)
            mids = [jnp.zeros((128, 128), f32) for _ in range(3)]
            for b in range(blocks):
                total = None
                for s in range(spans):
                    j = b - (spans - 1) + s
                    if 0 <= j < keys // 128:
                        term = slope[head, pl.ds(128 * j, 128), pl.ds(128 * s, 128)].astype(f32)
                        total = term if total is None else total + term
                wide[pl.ds(128 * b, 128), :] = total
                folded = total.reshape(16, 8, 128).sum(axis=0)
                low = low + jnp.where(b < first - 1, folded, 0.0)
                high = high + jnp.where(b > first + 1, folded, 0.0)
            line = pl.ds(2 * step + head, 1)
            for n in range(3):
                near = wide[pl.ds(pl.multiple_of(128 * (first - 1 + n), 128), 128), :]
                diag[n, line, :] = diagonals(near)
            far[0, line, :] = jnp.sum(low, axis=0, keepdims=True)
            far[1, line, :] = jnp.sum(high, axis=0, keepdims=True)
        lanes = pl.ds(pl.multiple_of(128 * step, 128), 128)
        gq[:, lanes] = jnp.concatenate([parts[0][0][:64], parts[0][1][64:]], axis=0).T.astype(bf16)
        mask = lane_mask(keys, 0)
        gk[:, lanes] = jnp.where(mask, parts[1][0], parts[1][1]).astype(bf16)
        gv[:, lanes] = jnp.where(mask, parts[2][0], parts[2][1]).astype(bf16)

    @pl.when(step == pairs)
    def _():
        mine = pl.ds(pl.multiple_of(g.core * rows, rows), rows)
        other = pl.ds(pl.multiple_of((1 - g.core) * rows, rows), rows)
        copies = [pltpu.make_async_remote_copy(a.at[other, :], b, s_kv.at[k], r_kv.at[k], device_id=mate, device_id_type=MESH)
                  for k, (a, b) in enumerate(((gk, rk), (gv, rv)))]
        for copy in copies:
            copy.start()
        square_grad(gq[...], 0)
        total = dot_of(gq[...], wq_ref[...], NT)
        due(1)
        for k, (a, b, w) in enumerate(((gk, rk, wk_ref), (gv, rv, wv_ref))):
            copies[k].wait()
            low = (a[mine, :].astype(f32) + b[...].astype(f32)).astype(bf16)
            b[...] = low
            square_grad(low, (k + 1) * square)
            total = total + dot_of(low, w[...], NT)
            due(2)
        edge().wait()
        for k in range(late.count):
            late.step(0, k)
        due(2)
        x = x_ref[...].astype(f32)
        scale = lax.rsqrt(jnp.mean(x * x, axis=1, keepdims=True) + 1e-06)
        unit = x * scale
        gain_row = jnp.sum(total * unit, axis=0, keepdims=True)
        c1 = total * gain_ref[...].astype(f32)
        ghid_copy().wait()
        gtok = gtok_out[...] + scale * (c1 - unit * jnp.mean(c1 * unit, axis=1, keepdims=True))
        gtok_out[...] = gtok

        @pl.when(moved)
        def _():
            gq[...] = gtok.astype(bf16)
            gt_copy().start()

        for k in range(late.count):
            late.step(1, k)
        due(2, True)

        tail = ends.mine(0)
        tail[...] = jnp.zeros(tail.shape, f32)
        for r in range(width // 128):
            tail[r : r + 1, :] = gain_row[:, 128 * r : 128 * r + 128]
            tail[width // 128 + r : width // 128 + r + 1, :] = ggain_ref[:, 128 * r : 128 * r + 128]
        for r, line in enumerate(table_rows(diag, far, heads, buckets)):
            tail[2 * width // 128 + r : 2 * width // 128 + r + 1, :] = line
        for k in range(3):
            tail[16 + k * count : 16 + (k + 1) * count, :] = jnp.where(place == count - 1, halo[k], 0.0)
        ends.start(0)
        for n in range(3):
            due(1, True)
            found = ends.done(n)
            ends.mine(n + 1)[...] = found
            ends.start(n + 1)
        due(len(pending), True)
        found = ends.done(3)
        grads = jnp.concatenate([found[:16], jnp.zeros((count - 16, 128), f32)], axis=0)
        last = [found[16 + k * count : 16 + (k + 1) * count] for k in range(3)]
        ftail[...] = adam_step(grads, *last)[2].astype(bf16)
        rest_copy = pltpu.make_async_copy(ftail, copy_out.at[pl.ds(stride * count, count), :], lsem.at[0])
        rest_copy.start()
        halo_copy().wait()
        summed[pl.ds(0, count), :] = jnp.zeros((count, 128), f32)

        def renew(job):
            job.collect()

            @pl.when(place == count - 1)
            def _():
                summed[pl.ds(count + stride, count), :] = grads

            renewed[pl.ds(0, count), :] = adam_step(summed[pl.ds(place, count), :], *[halo_in[k] for k in range(3)])[2]
            for start in range(0, shard, 216):
                size = min(216, shard - start)
                part = pl.ds(start, size)
                own = summed[pl.ds(place + count + start, size), :]
                one, two, new = adam_step(own, m1_ref[part, :], m2_ref[part, :], ma_ref[part, :])
                gshard_out[part, :] = own
                m1_out[part, :] = one
                m2_out[part, :] = two
                ma_out[part, :] = new
                renewed[pl.ds(count + start, size), :] = new
            for start in range(0, stride, stride // 8):
                fresh[pl.ds(start, stride // 8), :] = renewed[pl.ds(start + count - place, stride // 8), :].astype(bf16)

        own = range(spread.parts)

        def open_own():
            spread.begin()
            for k in own:
                spread.step(0, k)

        @pl.when(owner)
        def _():
            renew(early)

        @pl.when(jnp.logical_not(owner))
        def _():
            renew(late)

        open_own()
        for n in range(spread.count + 2):
            for stage in (0, 1, 2):
                k = n - stage
                if 0 <= k < spread.count and (stage, k) not in [(0, k) for k in own]:
                    spread.step(stage, k)
        early.finish()
        late.finish()
        spread.finish()
        rest_copy.wait()

        @pl.when(moved)
        def _():
            gt_copy().wait()
            gtok_out[...] = gt_in[...].astype(f32)


def back(grid, heads, buckets, query, keys_all, values_all, grad_mixed, mixed, prob, normed, x, grad_hidden, gain,
         wq, wk, wv, ggain, moment_one, moment_two, master, flat, collective_id):
    rows, width = query.shape
    span = keys_all.shape[0]
    pairs = width // 128
    shard = master.shape[0]
    count = grid.devices
    stride, window = shard - 1, shard - 1 + count
    cut = grid.planes // 4
    late_rows = 3 * width * width // 128
    early = Scatter(grid, cut, grid.planes - cut, stride, window, late_rows, False)
    late = Scatter(grid, 0, cut, stride, window, 0, True)
    spread = Gather(grid, stride)
    ends = TailSum(grid, 16 + 3 * count)
    at = lambda s: jnp.minimum(s, pairs - 1)
    tall = lambda n: pl.BlockSpec((n, 128), lambda s: (0, at(s)))
    dma = pltpu.SemaphoreType.DMA
    state = (shard, 128)
    return pl.pallas_call(
        functools.partial(back_kernel, grid, 256, early, late, ends, spread, heads, buckets),
        grid=(pairs + 1,),
        in_specs=[tall(rows), tall(span), tall(span), tall(rows), tall(rows),
                  pl.BlockSpec((2, span, rows), lambda s: (at(s), 0, 0)),
                  once((rows, width)), once((rows, width)), pl.BlockSpec(memory_space=pl.ANY), once((1, width)),
                  once((width, width)), once((width, width)), once((width, width)),
                  once((1, width)), once(state), once(state), once(state),
                  pl.BlockSpec(memory_space=pl.ANY)],
        out_specs=[once((rows, width)), once(state), once(state), once(state), once(state),
                   pl.BlockSpec(memory_space=pl.ANY)],
        out_shape=[jax.ShapeDtypeStruct(s, t) for s, t in (
            ((rows, width), f32), (state, f32), (state, f32), (state, f32), (state, f32),
            (((stride + 1) * count, 128), bf16))],
        scratch_shapes=early.scratch() + late.scratch() + ends.scratch() + spread.scratch() + [
            pltpu.VMEM((2, span, rows), bf16), pltpu.VMEM((rows, width), bf16),
            pltpu.VMEM((span, width), bf16), pltpu.VMEM((span, width), bf16),
            pltpu.VMEM((rows, width), bf16), pltpu.VMEM((rows, width), bf16),
            pltpu.VMEM((late_rows + count, 128), bf16), pltpu.VMEM((late_rows // 9, 128), f32),
            pltpu.VMEM((3, 16, 256), f32), pltpu.VMEM((2, 16, 128), f32),
            pltpu.VMEM((rows, width), bf16),
            pltpu.VMEM((3, count, 128), f32), pltpu.VMEM((3, count, 128), f32),
            pltpu.VMEM((count + window, 128), f32), pltpu.VMEM((count + shard + 7, 128), f32),
            pltpu.VMEM((stride, 128), bf16), pltpu.VMEM((count, 128), bf16),
            dma((2,)), dma((2,)), dma((2,)), dma((2,)), dma((2,))],
        compiler_params=pltpu.CompilerParams(collective_id=collective_id, has_side_effects=True, vmem_limit_bytes=62 << 20),
    )(query, keys_all, values_all, grad_mixed, mixed, prob, normed, x, grad_hidden, gain, wq, wk, wv, ggain,
      moment_one, moment_two, master, flat)


def per_device(tokens, lengths, cotangent, w_query, w_keys, w_values, w_output, w_gate, w_up, w_down,
               gain_attn, gain_ffn, bias_table, master, moment_one, moment_two):
    rows, width = tokens.shape
    grid = Grid(lax.axis_size("dp")).here()
    span = rows * lax.axis_size("group")
    count = grid.devices
    first_row = grid.core * rows
    near = near_rows(bias_table, rows, span, first_row)
    lens = jnp.broadcast_to(lengths.reshape(1, 1), (8, 128))
    gain_one, gain_two = gain_attn.reshape(1, width), gain_ffn.reshape(1, width)
    x, cot, lens, normed, query, keys_all, values_all, mixed, prob = front(
        grid, tokens, cotangent, lens, gain_one, w_query, w_keys, w_values, near, 1)
    layer_out, grad_hidden, grad_mixed, grad_gain_ffn, flat = ffn(
        lens, x, mixed, cot, gain_two, w_output, w_gate, w_up, w_down, count, 3)
    grad_tokens, grad_shard, moment_one_new, moment_two_new, master_new, fresh_copy = back(
        grid, bias_table.shape[1], bias_table.shape[0], query, keys_all, values_all, grad_mixed, mixed, prob, normed, x,
        grad_hidden, gain_one, w_query, w_keys, w_values, grad_gain_ffn, moment_one, moment_two, master, flat, 2)
    return (layer_out, grad_tokens, grad_shard, moment_one_new, moment_two_new, master_new, fresh_copy)


def solution(mesh):
    both = P(("dp", "group"), None)
    return jax.shard_map(
        per_device,
        mesh=mesh,
        in_specs=(both, P("dp"), both) + (P(),) * 10 + (both,) * 3,
        out_specs=(both,) * 6 + (P(),),
        check_vma=False,
    )
```

```python
import functools
import jax
import jax.numpy as jnp
from jax import lax
from jax.experimental import pallas as pl
from jax.experimental.pallas import tpu as pltpu
from jax.sharding import PartitionSpec as P

MESH = pl.DeviceIdType.MESH
bf16, f32 = jnp.bfloat16, jnp.float32
NN = (((1,), (0,)), ((), ()))
NT = (((1,), (1,)), ((), ()))
TN = (((0,), (0,)), ((), ()))
root_half = 0.7978845608028654


class Grid:
    def __init__(self, dp):
        half = dp // 2
        self.X = 1
        while self.X * self.X * 4 <= half:
            self.X *= 2
        self.planes = half // self.X
        self.devices = dp * 2
        self.swap = self.X == 2

    def here(self):
        return Grid(self.devices // 2).place()

    def place(self):
        dp = lax.axis_index("dp")
        self.core = lax.rem(dp, 2)
        self.x = lax.rem(lax.div(dp, 2), self.X)
        self.plane = lax.div(dp, 2 * self.X)
        self.y = lax.axis_index("group")
        self.flip = self.core if self.swap else 0
        if self.swap:
            self.a = jnp.where(self.core == 0, self.x, self.y)
            self.b = jnp.where(self.core == 0, self.y, self.x)
        else:
            self.a, self.b = self.x, self.y
        return self

    def xy(self, a, b):
        if not self.swap:
            return a, b
        return jnp.where(self.core == 0, a, b), jnp.where(self.core == 0, b, a)

    def device(self, plane=None, a=None, b=None, core=None):
        plane = self.plane if plane is None else plane
        a = self.a if a is None else a
        b = self.b if b is None else b
        x, y = self.xy(a, b)
        core = self.core if core is None else core
        return ((plane * self.X + x) * 2 + core, y)

    def index(self, plane, x, core, y):
        return ((plane * self.X + x) * 2 + core) * 2 + y

    def partners(self):
        found = [self.device(core=1 - self.core), self.device(b=1 - self.b)]
        found += [self.device(a=lax.rem(self.a + d, self.X)) for d in range(1, self.X)]
        found += [self.device(plane=lax.rem(self.plane + d, self.planes)) for d in range(1, self.planes)]
        return found


def enter(partners):
    barrier = pltpu.get_barrier_semaphore()
    for one in partners:
        pl.semaphore_signal(barrier, inc=1, device_id=one, device_id_type=MESH)
    pl.semaphore_wait(barrier, len(partners))


def add_rows(out, terms, rows, block):
    @pl.loop(0, rows // block)
    def _(step):
        part = pl.ds(pl.multiple_of(step * block, block), block)
        total = terms[0][part, :].astype(f32)
        for term in terms[1:]:
            total = total + term[part, :].astype(f32)
        out[part, :] = total.astype(out.dtype)


def block_of(rows):
    for tiles in range(12, 0, -1):
        if rows % (16 * tiles) == 0:
            return 16 * tiles


class Scatter:
    def __init__(self, grid, first, planes, stride, window, base, tree):
        self.g, self.first, self.owners, self.stride, self.window = grid, first, planes, stride, window
        self.base, self.tree = base, tree
        self.parts = 2 if window % 32 == 0 else 1
        self.rows = window // self.parts
        self.count = planes * self.parts
        self.levels = grid.planes.bit_length() - 1
        self.ahead = 6

    def scratch(self):
        g, n, w = self.g, self.count, self.rows
        dma = pltpu.SemaphoreType.DMA
        lines = self.levels * self.owners if self.tree else g.planes - 1
        return [
            pltpu.VMEM((n, g.X, 2, w, 128), bf16),
            pltpu.VMEM((n, g.X, 2, w, 128), bf16),
            pltpu.VMEM((n, g.X - 1, 2, w, 128), bf16),
            pltpu.VMEM((n, w, 128), bf16),
            pltpu.VMEM((lines, self.parts, w, 128), bf16),
            dma((n, g.X, 2)), dma((n, g.X, 2)), dma((n, g.X, 2)),
            dma((n, g.X - 1, 2)), dma((n, g.X - 1, 2)),
            dma((n,)), dma((n,)), dma((n,)), dma((lines, self.parts)),
        ]

    def bind(self, flat, out, scratch):
        (self.own, self.r1, self.r2, self.r3, self.r4, self.lsem, self.s1, self.q1, self.s2,
         self.q2, self.s3, self.q3, self.s4, self.q4) = scratch
        self.flat, self.out, self.g = flat, out, self.g.here()

    def plane_of(self, k):
        n, j = self.owners, k // self.parts
        g = self.g
        return self.first + lax.rem(g.plane - self.first + n + 1 + j, n)

    def add(self, out, terms):
        add_rows(out, terms, self.rows, block_of(self.rows))

    def copies0(self, k):
        g = self.g
        q = self.plane_of(k)
        shift = k % self.parts * self.rows - self.base
        for x in range(g.X):
            for y in range(2):
                there = pl.multiple_of(self.stride * g.index(q, x, 1 - g.core, y) + shift, 16)
                here = pl.multiple_of(self.stride * g.index(q, x, g.core, y) + shift, 16)
                yield (
                    pltpu.make_async_remote_copy(
                        self.flat.at[pl.ds(there, self.rows), :], self.r1.at[k, x, y],
                        self.s1.at[k, x, y], self.q1.at[k, x, y],
                        device_id=g.device(core=1 - g.core), device_id_type=MESH),
                    pltpu.make_async_copy(
                        self.flat.at[pl.ds(here, self.rows), :], self.own.at[k, x, y], self.lsem.at[k, x, y]),
                    x, y)

    def copies1(self, k):
        g = self.g
        for d in range(1, g.X):
            a = lax.rem(g.a + d, g.X)
            for b in range(2):
                x, y = g.xy(a, b)
                yield pltpu.make_async_remote_copy(
                    self.own.at[k, x, y], self.r2.at[k, d - 1, b], self.s2.at[k, d - 1, b], self.q2.at[k, d - 1, b],
                    device_id=g.device(a=a), device_id_type=MESH)

    def copy2(self, k):
        g = self.g
        x, y = g.xy(g.a, 1 - g.b)
        return pltpu.make_async_remote_copy(
            self.own.at[k, x, y], self.r3.at[k], self.s3.at[k], self.q3.at[k],
            device_id=g.device(b=1 - g.b), device_id_type=MESH)

    def distance(self, k):
        return lax.rem(self.g.plane - self.plane_of(k) + self.g.planes, self.g.planes)

    def copy3(self, k, line, plane):
        g = self.g
        part = k % self.parts
        return pltpu.make_async_remote_copy(
            self.own.at[k, g.x, g.y], self.r4.at[line, part], self.s4.at[k], self.q4.at[line, part],
            device_id=g.device(plane=plane), device_id_type=MESH)

    def climb(self, k, level, wait):
        far = self.distance(k)
        line = level * self.owners + self.plane_of(k) - self.first

        @pl.when(lax.rem(far, 2 << level) == 1 << level)
        def _():
            copy = self.copy3(k, line, lax.rem(self.g.plane - (1 << level) + self.g.planes, self.g.planes))
            copy.wait_send() if wait else copy.start()

    def step(self, stage, k):
        g = self.g
        if stage == 0:
            for far, near, x, y in self.copies0(k):
                far.start()
                near.start()
        elif stage == 1:
            for far, near, x, y in self.copies0(k):
                near.wait()
                far.wait()
                self.add(self.own.at[k, x, y], [self.own.at[k, x, y], self.r1.at[k, x, y]])
            if k < self.ahead:
                for copy in self.copies1(k):
                    copy.start()
        elif stage == 2:
            for copy in self.copies1(k):
                copy.wait()
            if k + self.ahead < self.count:
                for copy in self.copies1(k + self.ahead):
                    copy.start()
            for b in (1 - g.b, g.b):
                x, y = g.xy(g.a, b)
                mine = self.own.at[k, x, y]
                self.add(mine, [mine] + [self.r2.at[k, d, b] for d in range(g.X - 1)])
                if b is not g.b:
                    self.copy2(k).start()
        elif stage == 3:
            self.copy2(k).wait()
            mine = self.own.at[k, g.x, g.y]
            self.add(mine, [mine, self.r3.at[k]])
            if self.tree:
                self.climb(k, 0, False)
            else:
                far = self.distance(k)

                @pl.when(far > 0)
                def _():
                    self.copy3(k, far - 1, self.plane_of(k)).start()
        else:
            level = stage - 4
            far = self.distance(k)
            mine = self.own.at[k, g.x, g.y]
            line = level * self.owners + self.plane_of(k) - self.first

            @pl.when(lax.rem(far, 2 << level) == 0)
            def _():
                self.copy3(k, line, self.plane_of(k)).wait_recv()
                self.add(mine, [mine, self.r4.at[line, k % self.parts]])

            if level + 1 < self.levels:
                self.climb(k, level + 1, False)

    def finish(self):
        g = self.g
        for k in range(self.count):
            if self.tree:
                for level in range(self.levels):
                    self.climb(k, level, True)
            else:
                @pl.when(self.distance(k) > 0)
                def _():
                    self.copy3(k, 0, self.plane_of(k)).wait_send()

    def collect(self):
        g = self.g
        for part in range(self.parts):
            k = (self.owners - 1) * self.parts + part
            terms = [self.own.at[k, g.x, g.y]]
            if not self.tree:
                for d in range(g.planes - 1):
                    self.copy3(k, d, lax.rem(g.plane + 1 + d, g.planes)).wait_recv()
                    terms.append(self.r4.at[d, part])
            self.add(self.out.at[pl.ds(part * self.rows, self.rows), :], terms)


class Gather:
    def __init__(self, grid, stride):
        self.g, self.stride = grid, stride
        self.parts = 3 if stride % 48 == 0 else 1
        self.rows = stride // self.parts
        self.count = grid.planes * self.parts

    def scratch(self):
        dma = pltpu.SemaphoreType.DMA
        n, X, planes, parts = self.count, self.g.X, self.g.planes, self.parts
        return [dma((parts,)), dma((2 * planes - 1, parts)), dma((planes, parts)), dma((n,)), dma((n,)),
                dma((n, X - 1, 2)), dma((n, X - 1, 2)), dma((n, X, 2)), dma((n, X, 2))]

    def bind(self, fresh, out, scratch):
        self.lsem, self.s0, self.q0, self.s1, self.q1, self.s2, self.q2, self.s3, self.q3 = scratch
        self.fresh, self.out, self.g = fresh, out, self.g.here()

    def plane_of(self, k):
        g = self.g
        j = k // self.parts
        if g.planes == 4:
            one = jnp.where(g.plane == 0, (0, 1, 2, 3)[j], (1, 2, 0, 3)[j])
            other = jnp.where(g.plane == 2, (2, 1, 3, 0)[j], (3, 2, 1, 0)[j])
            return jnp.where(g.plane < 2, one, other)
        up = g.planes - 1 - g.plane
        return jnp.where(j <= up, g.plane + j, g.plane - (j - up))

    def part(self, q, x, core, y, part):
        g = self.g
        start = self.stride * g.index(q, x, core, y) + part * self.rows
        return self.out.at[pl.ds(pl.multiple_of(start, 16), self.rows), :]

    def first(self, part):
        g = self.g
        return pltpu.make_async_copy(
            self.fresh.at[pl.ds(part * self.rows, self.rows), :], self.part(g.plane, g.x, g.core, g.y, part), self.lsem.at[part])

    def send0(self, part, way):
        g = self.g
        rows = self.part(g.plane, g.x, g.core, g.y, part)
        slot = way + g.planes - 1
        return pltpu.make_async_remote_copy(
            self.fresh.at[pl.ds(part * self.rows, self.rows), :], rows, self.s0.at[slot, part], self.q0.at[g.plane, part],
            device_id=g.device(plane=jnp.clip(g.plane + way, 0, g.planes - 1)), device_id_type=MESH)

    def came0(self, q, part):
        g = self.g
        rows = self.part(q, g.x, g.core, g.y, part)
        return pltpu.make_async_remote_copy(
            rows, rows, self.s0.at[0, part], self.q0.at[q, part], device_id=g.device(plane=q), device_id_type=MESH)

    def reach(self, far, wait):
        g = self.g
        for part in range(self.parts):
            for way in (-far, far):
                @pl.when(jnp.logical_and(g.plane + way >= 0, g.plane + way < g.planes))
                def _():
                    copy = self.send0(part, way)
                    copy.wait_send() if wait else copy.start()

    def send1(self, k):
        g = self.g
        rows = self.part(self.plane_of(k), g.x, g.core, g.y, k % self.parts)
        return pltpu.make_async_remote_copy(
            rows, rows, self.s1.at[k], self.q1.at[k], device_id=g.device(b=1 - g.b), device_id_type=MESH)

    def send2(self, k):
        g = self.g
        for d in range(1, g.X):
            for b in range(2):
                x, y = g.xy(g.a, (g.b, 1 - g.b)[b])
                rows = self.part(self.plane_of(k), x, g.core, y, k % self.parts)
                yield pltpu.make_async_remote_copy(
                    rows, rows, self.s2.at[k, d - 1, b], self.q2.at[k, d - 1, b],
                    device_id=g.device(a=lax.rem(g.a + d, g.X)), device_id_type=MESH)

    def send3(self, k):
        g = self.g
        for x in range(g.X):
            for y in range(2):
                rows = self.part(self.plane_of(k), x, g.core, y, k % self.parts)
                yield pltpu.make_async_remote_copy(
                    rows, rows, self.s3.at[k, x, y], self.q3.at[k, x, y],
                    device_id=g.device(core=1 - g.core), device_id_type=MESH)

    def begin(self):
        for far in range(1, self.g.planes):
            self.reach(far, False)
        for part in range(self.parts):
            self.first(part).start()

    def step(self, stage, k):
        g = self.g
        q, part = self.plane_of(k), k % self.parts
        if stage == 0:
            @pl.when(q == g.plane)
            def _():
                self.first(part).wait()

            @pl.when(q != g.plane)
            def _():
                self.came0(q, part).wait_recv()

            self.send1(k).start()
            for n, copy in enumerate(self.send2(k)):
                if n % 2 == 0:
                    copy.start()
        elif stage == 1:
            self.send1(k).wait_recv()
            for n, copy in enumerate(self.send2(k)):
                if n % 2 == 1:
                    copy.start()
        else:
            for copy in self.send2(k):
                copy.wait_recv()
            for copy in self.send3(k):
                copy.start()

    def finish(self):
        for far in range(1, self.g.planes):
            self.reach(far, True)
        for k in range(self.count):
            self.send1(k).wait_send()
            for copy in self.send2(k):
                copy.wait_send()
            for copy in self.send3(k):
                copy.wait()


def lane_mask(rows, head):
    lane = lax.broadcasted_iota(jnp.int32, (rows, 128), 1)
    return (lane < 64) if head == 0 else (lane >= 64)


far_steps = (8, 12, 16, 23, 32, 46, 64, 91)


def bucket_index(offset):
    distance = jnp.abs(offset)
    passed = sum((distance >= one).astype(jnp.int32) for one in far_steps)
    inside = jnp.where(distance < 8, distance, 7 + passed)
    return inside + 16 * (offset > 0).astype(jnp.int32)


def near_rows(table, rows, span, first_row):
    spans = rows // 128
    blocks = span // 128 + spans
    offset = (
        128 * (jnp.arange(blocks, dtype=jnp.int32)[:, None] - (spans - 1))
        - jnp.arange(128, dtype=jnp.int32)[None, :] - first_row)
    onehot = (bucket_index(offset)[None] == jnp.arange(table.shape[0], dtype=jnp.int32)[:, None, None])
    return jnp.sum(jnp.where(onehot[:, None], table.astype(f32)[:, :, None, None], 0.0), axis=0)


def dot_of(left, right, dims):
    return lax.dot_general(left, right, dims, preferred_element_type=f32)


def flatten_into(value, wide, out, first):
    rows, columns = value.shape
    parts = columns // 128
    for part in range(parts):
        wide[pl.ds(part, rows, stride=parts), :] = value[:, 128 * part : 128 * part + 128]
    size = rows * parts
    out[pl.ds(first, size), :] = wide[pl.ds(0, size), :].astype(bf16)


def ffn_kernel(steps, tall, bases, length, x_ref, mixed_ref, cot_ref, gain_ref, wo_ref, wg_ref, wu_ref, wd_ref,
               out_ref, ghid_ref, gmix_ref, ggain_ref, flat_ref,
               flat, wide, hidden, nf, nft, gout, gate_low, up_low, out_sum, gnf_sum, sems, lo_send, lo_in, turn):
    step = pl.program_id(0)
    rows, width = x_ref.shape
    chunk = wg_ref.shape[1]
    o_base, g_base, u_base, d_base, end = bases
    dp, y = lax.axis_index("dp"), lax.axis_index("group")
    core = lax.rem(dp, 2)
    twin = (dp - core + y, core)
    moved = core != y
    lo_copy = lambda: pltpu.make_async_remote_copy(
        lo_send, lo_in, turn.at[0], turn.at[1], device_id=twin, device_id_type=MESH)

    @pl.when(jnp.logical_and(step == 0, moved))
    def _():
        barrier = pltpu.get_barrier_semaphore()
        pl.semaphore_signal(barrier, inc=1, device_id=twin, device_id_type=MESH)

    @pl.when(jnp.logical_and(step == steps - 1, moved))
    def _():
        pl.semaphore_wait(pltpu.get_barrier_semaphore(), 1)

    @pl.when(step == 0)
    def _():
        place = lax.broadcasted_iota(jnp.int32, (rows, width), 0) + lax.rem(lax.axis_index("dp"), 2) * rows
        cot = cot_ref[...]
        gout[...] = jnp.where(place < length[0:1, 0:1], cot, jnp.zeros_like(cot))
        total = x_ref[...].astype(f32) + dot_of(mixed_ref[...], wo_ref[...], NN)
        hidden[...] = total
        scale = lax.rsqrt(jnp.mean(total * total, axis=1, keepdims=True) + 1e-06)
        normed = (total * scale * gain_ref[...].astype(f32)).astype(bf16)
        nf[...] = normed
        nft[...] = normed.T
        out_sum[...] = total
        gnf_sum[...] = jnp.zeros_like(gnf_sum)
        flat[pl.ds(end, flat.shape[0] - end), :] = jnp.zeros((flat.shape[0] - end, 128), bf16)

    @pl.when(step < steps)
    def _():
        gate = dot_of(nf[...], wg_ref[...], NN)
        up = dot_of(nf[...], wu_ref[...], NN)
        ginner = dot_of(gout[...], wd_ref[...], NT)
        square = gate * gate
        th = jnp.tanh(root_half * (gate + 0.044715 * gate * square))
        half = 0.5 * (1.0 + th)
        act = gate * half
        slope = half + 0.5 * gate * (1.0 - th * th) * (root_half * (1.0 + 3 * 0.044715 * square))
        inner = (act * up).astype(bf16)
        ggate = (ginner * up * slope).astype(bf16)
        gup = (ginner * act).astype(bf16)
        gate_low[:, pl.ds(pl.multiple_of(step * chunk, chunk), chunk)] = ggate
        up_low[:, pl.ds(pl.multiple_of(step * chunk, chunk), chunk)] = gup
        out_sum[...] += dot_of(inner, wd_ref[...], NN)
        gnf_sum[...] += dot_of(ggate, wg_ref[...], NT) + dot_of(gup, wu_ref[...], NT)
        size = chunk * (width // 128)
        flatten_into(dot_of(inner, gout[...], TN), wide, flat, pl.multiple_of(d_base + step * size, 16))
        part = pl.ds(pl.multiple_of(d_base + step * size, 16), size)
        pltpu.make_async_copy(flat.at[part, :], flat_ref.at[part, :], sems.at[step]).start()

    @pl.when(step == steps - 1)
    def _():
        low = out_sum[...].astype(bf16)
        out_ref[...] = low

        @pl.when(moved)
        def _():
            lo_send[...] = low
            lo_copy().start()

        total = hidden[...]
        scale = lax.rsqrt(jnp.mean(total * total, axis=1, keepdims=True) + 1e-06)
        unit = total * scale
        grad = gnf_sum[...]
        ggain_ref[...] = jnp.sum(grad * unit, axis=0, keepdims=True)
        c2 = grad * gain_ref[...].astype(f32)
        ghid = gout[...].astype(f32) + scale * (c2 - unit * jnp.mean(c2 * unit, axis=1, keepdims=True))
        ghid_ref[...] = ghid
        branch = ghid.astype(bf16)
        gmix_ref[...] = dot_of(branch, wo_ref[...], NT).astype(bf16)
        size = width * width // 128
        flatten_into(dot_of(mixed_ref[...], branch, TN), wide, flat, o_base)
        part = pl.ds(o_base, size)
        pltpu.make_async_copy(flat.at[part, :], flat_ref.at[part, :], sems.at[steps]).start()

    turns = width // tall
    for k, (low, base) in enumerate(((gate_low, g_base), (up_low, u_base))):
        @pl.when(jnp.logical_and(step >= steps + k * turns, step < steps + (k + 1) * turns))
        def _():
            turn = step - steps - k * turns
            columns = low.shape[1]
            size = tall * columns // 128
            value = dot_of(nft[pl.ds(pl.multiple_of(turn * tall, tall), tall), :], low[...], NN)
            first = pl.multiple_of(base + turn * size, 16)
            flatten_into(value, wide, flat, first)
            pltpu.make_async_copy(flat.at[pl.ds(first, size), :], flat_ref.at[pl.ds(first, size), :], sems.at[step + 1]).start()

    @pl.when(step == steps + 2 * turns - 1)
    def _():
        rest = flat.shape[0] - end
        last = pltpu.make_async_copy(flat.at[pl.ds(end, rest), :], flat_ref.at[pl.ds(end, rest), :], sems.at[steps + 2 * turns + 1])
        last.start()
        for s in range(steps):
            size = chunk * (width // 128)
            part = pl.ds(d_base + s * size, size)
            pltpu.make_async_copy(flat.at[part, :], flat_ref.at[part, :], sems.at[s]).wait()
        part = pl.ds(o_base, width * width // 128)
        pltpu.make_async_copy(flat.at[part, :], flat_ref.at[part, :], sems.at[steps]).wait()
        for k, base in enumerate((g_base, u_base)):
            size = tall * gate_low.shape[1] // 128
            for turn in range(turns):
                part = pl.ds(base + turn * size, size)
                pltpu.make_async_copy(flat.at[part, :], flat_ref.at[part, :], sems.at[steps + k * turns + turn + 1]).wait()
        last.wait()

        @pl.when(moved)
        def _():
            lo_copy().wait()
            out_ref[...] = lo_in[...]


def ffn(length, x, mixed, cot, gain, wo, wg, wu, wd, pad_rows, collective_id):
    rows, width = x.shape
    deep = wg.shape[1]
    chunk, tall = 256, 256
    steps = deep // chunk
    turns = width // tall
    square, oblong = width * width // 128, width * deep // 128
    bases = (0, square, square + oblong, square + 2 * oblong, square + 3 * oblong)
    total = bases[4] + pad_rows
    whole = lambda shape: pl.BlockSpec(shape, lambda s: (0, 0))
    at = lambda s: jnp.minimum(s, steps - 1)
    return pl.pallas_call(
        functools.partial(ffn_kernel, steps, tall, bases),
        grid=(steps + 2 * turns,),
        in_specs=[whole(length.shape), whole((rows, width)), whole((rows, width)), whole((rows, width)), whole((1, width)),
                  whole((width, width)),
                  pl.BlockSpec((width, chunk), lambda s: (0, at(s))),
                  pl.BlockSpec((width, chunk), lambda s: (0, at(s))),
                  pl.BlockSpec((chunk, width), lambda s: (at(s), 0))],
        out_specs=[whole((rows, width)), whole((rows, width)), whole((rows, width)), whole((1, width)),
                   pl.BlockSpec(memory_space=pl.ANY)],
        out_shape=[jax.ShapeDtypeStruct((rows, width), bf16), jax.ShapeDtypeStruct((rows, width), f32),
                   jax.ShapeDtypeStruct((rows, width), bf16), jax.ShapeDtypeStruct((1, width), f32),
                   jax.ShapeDtypeStruct((total, 128), bf16)],
        scratch_shapes=[
            pltpu.VMEM((total, 128), bf16), pltpu.VMEM((max(tall * deep, square * 128) // 128, 128), f32),
            pltpu.VMEM((rows, width), f32), pltpu.VMEM((rows, width), bf16), pltpu.VMEM((width, rows), bf16),
            pltpu.VMEM((rows, width), bf16), pltpu.VMEM((rows, deep), bf16), pltpu.VMEM((rows, deep), bf16),
            pltpu.VMEM((rows, width), f32), pltpu.VMEM((rows, width), f32),
            pltpu.SemaphoreType.DMA((steps + 2 * turns + 2,)),
            pltpu.VMEM((rows, width), bf16), pltpu.VMEM((rows, width), bf16), pltpu.SemaphoreType.DMA((2,))],
        compiler_params=pltpu.CompilerParams(collective_id=collective_id, has_side_effects=True, vmem_limit_bytes=56 << 20),
    )(length, x, mixed, cot, gain, wo, wg, wu, wd)


def near_toeplitz(y_ref, head, b):
    near = jnp.concatenate([y_ref[head, b : b + 1, :], y_ref[head, b + 1 : b + 2, :]], axis=1)
    return pltpu.roll(jnp.broadcast_to(near, (128, 256)), 0, 1, stride=1, stride_axis=0)[:, :128]


def front_kernel(grid, chunk, tok_ref, cot_ref, len_ref, gain_ref, wq_ref, wk_ref, wv_ref, y_ref,
                 x_out, cot_out, len_out, normed_out, q_out, k_out, v_out, mixed_out, prob_ref,
                 xs, cs, ls, keys, values, bias, score, sems, s_kv, r_kv):
    g = grid.here()
    pair = pl.program_id(0)
    rows, width = tok_ref.shape
    span = keys.shape[0]
    spans = rows // 128
    blocks = span // 128 + spans - 1
    mate = g.device(core=1 - g.core)
    dp = lax.axis_index("dp")
    twin = (dp - g.core + g.y, g.core)
    moved = g.core != g.y
    first = pl.multiple_of(g.core * rows, rows)

    def move(k, begin):
        src, dst = ((tok_ref, xs), (cot_ref, cs))[k]

        @pl.when(moved)
        def _():
            far = pltpu.make_async_remote_copy(
                src, dst, sems.at[2 * k], sems.at[2 * k + 1], device_id=twin, device_id_type=MESH)
            far.start() if begin else far.wait()

        @pl.when(jnp.logical_not(moved))
        def _():
            near = pltpu.make_async_copy(src, dst, sems.at[2 * k + 1])
            near.start() if begin else near.wait()

    lens_copy = lambda: pltpu.make_async_remote_copy(len_ref, ls, sems.at[4], sems.at[5], device_id=mate, device_id_type=MESH)

    def swaps():
        part = pl.ds(first, rows)
        for k, buf in enumerate((keys, values)):
            yield pltpu.make_async_remote_copy(buf.at[part, :], buf.at[part, :], s_kv.at[k], r_kv.at[k], device_id=mate, device_id_type=MESH)

    @pl.when(pair == 0)
    def _():
        barrier = pltpu.get_barrier_semaphore()
        pl.semaphore_signal(barrier, inc=1, device_id=mate, device_id_type=MESH)

        @pl.when(moved)
        def _():
            pl.semaphore_signal(barrier, inc=1, device_id=twin, device_id_type=MESH)

        pl.semaphore_wait(barrier, jnp.where(moved, 2, 1))
        move(0, True)
        move(1, True)
        lens = lens_copy()
        lens.start()
        move(0, False)
        wide = xs[...].astype(f32)
        normed = (wide * lax.rsqrt(jnp.mean(wide * wide, axis=1, keepdims=True) + 1e-06)
                  * gain_ref[...].astype(f32)).astype(bf16)
        x_out[...] = xs[...]
        normed_out[...] = normed
        keys[pl.ds(first, rows), :] = dot_of(normed, wk_ref[...], NN).astype(bf16)
        values[pl.ds(first, rows), :] = dot_of(normed, wv_ref[...], NN).astype(bf16)
        for copy in swaps():
            copy.start()
        q_out[...] = dot_of(normed, wq_ref[...], NN).astype(bf16)
        lens.wait()
        len_out[...] = jnp.where(moved, ls[...], len_ref[...])
        for copy in swaps():
            copy.wait()

    lanes = pl.ds(pl.multiple_of(128 * pair, 128), 128)
    live = len_out[0:1, 0:1]
    for head in range(2):
        for b in range(blocks):
            bias[head, pl.ds(128 * b, 128), :] = near_toeplitz(y_ref, head, b)
    halves = []
    for head in range(2):
        query = q_out[:, lanes]
        query = jnp.where(lane_mask(rows, head), query, jnp.zeros_like(query))
        top = jnp.full((1, rows), -jnp.inf, f32)
        for c in range(span // chunk):
            part = pl.ds(chunk * c, chunk)
            raw = dot_of(keys[part, lanes], query, NT)
            added = jnp.concatenate(
                [bias[head, pl.ds(128 * (spans - 1 - s) + chunk * c, chunk), :] for s in range(spans)], axis=1)
            place = lax.broadcasted_iota(jnp.int32, (chunk, rows), 0) + chunk * c
            raw = jnp.where(place < live, raw + added, -jnp.inf)
            score[head, part, :] = raw
            top = jnp.maximum(top, jnp.max(raw, axis=0, keepdims=True))
        total = jnp.zeros((1, rows), f32)
        for c in range(span // chunk):
            part = pl.ds(chunk * c, chunk)
            grown = jnp.exp(score[head, part, :] - top)
            score[head, part, :] = grown
            total = total + jnp.sum(grown, axis=0, keepdims=True)
        inverse = 1.0 / total
        for c in range(span // chunk):
            part = pl.ds(chunk * c, chunk)
            prob_ref[head, part, :] = (score[head, part, :] * inverse).astype(bf16)
        halves.append(dot_of(values[:, lanes], prob_ref[head], TN))
    both = jnp.concatenate([halves[0][:64], halves[1][64:]], axis=0)
    mixed_out[:, lanes] = both.T.astype(bf16)

    @pl.when(pair == pl.num_programs(0) - 1)
    def _():
        k_out[...] = keys[...]
        v_out[...] = values[...]
        move(1, False)
        cot_out[...] = cs[...]


def once(shape):
    return pl.BlockSpec(shape, lambda s: (0,) * len(shape), pipeline_mode=pl.Buffered(1))


def front(grid, tokens, cot, lens, gain, wq, wk, wv, near, collective_id):
    rows, width = tokens.shape
    span, pairs, blocks = 2 * rows, width // 128, near.shape[1]
    row_shape, key_shape = (rows, width), (span, width)
    dma = pltpu.SemaphoreType.DMA
    return pl.pallas_call(
        functools.partial(front_kernel, grid, 256),
        grid=(pairs,),
        in_specs=[once(row_shape), once(row_shape), once(lens.shape), once((1, width)),
                  once((width, width)), once((width, width)), once((width, width)),
                  pl.BlockSpec((2, blocks, 128), lambda p: (p, 0, 0))],
        out_specs=[once(row_shape), once(row_shape), once(lens.shape), once(row_shape), once(row_shape),
                   once(key_shape), once(key_shape), once(row_shape),
                   pl.BlockSpec((2, span, rows), lambda p: (p, 0, 0))],
        out_shape=[jax.ShapeDtypeStruct(s, t) for s, t in (
            (row_shape, bf16), (row_shape, bf16), (lens.shape, jnp.int32), (row_shape, bf16), (row_shape, bf16),
            (key_shape, bf16), (key_shape, bf16), (row_shape, bf16), ((2 * pairs, span, rows), bf16))],
        scratch_shapes=[pltpu.VMEM(row_shape, bf16), pltpu.VMEM(row_shape, bf16), pltpu.VMEM(lens.shape, jnp.int32),
                        pltpu.VMEM(key_shape, bf16), pltpu.VMEM(key_shape, bf16),
                        pltpu.VMEM((2, 128 * (blocks - 1), 128), f32), pltpu.VMEM((2, span, rows), f32),
                        dma((6,)), dma((2,)), dma((2,))],
        compiler_params=pltpu.CompilerParams(collective_id=collective_id, has_side_effects=True, vmem_limit_bytes=56 << 20),
    )(tokens, cot, lens, gain, wq, wk, wv, near)


class TailSum:
    def __init__(self, grid, rows):
        self.g, self.rows = grid, rows
        self.sizes = (2, grid.X, 2, grid.planes)

    def scratch(self):
        dma = pltpu.SemaphoreType.DMA
        return [pltpu.VMEM((size, self.rows, 128), f32) for size in self.sizes] + [
            dma((sum(self.sizes),)), dma((sum(self.sizes),))]

    def bind(self, scratch):
        self.bufs, self.send, self.recv = scratch[:4], scratch[4], scratch[5]
        self.g = g = self.g.here()
        self.places = (g.core, g.a, g.b, g.plane)

    def mate(self, axis, place):
        g = self.g
        return (g.device(core=place), g.device(a=place), g.device(b=place), g.device(plane=place))[axis]

    def mine(self, axis):
        return self.bufs[axis].at[self.places[axis]]

    def copies(self, axis):
        base = sum(self.sizes[:axis])
        for d in range(1, self.sizes[axis]):
            there = lax.rem(self.places[axis] + d, self.sizes[axis])
            buf = self.bufs[axis]
            yield pltpu.make_async_remote_copy(
                buf.at[self.places[axis]], buf.at[self.places[axis]], self.send.at[base + d], self.recv.at[base + d],
                device_id=self.mate(axis, there), device_id_type=MESH)

    def start(self, axis):
        for copy in self.copies(axis):
            copy.start()

    def done(self, axis):
        for copy in self.copies(axis):
            copy.wait_send()
        base = sum(self.sizes[:axis])
        for d in range(1, self.sizes[axis]):
            behind = lax.rem(self.places[axis] - d + self.sizes[axis], self.sizes[axis])
            buf = self.bufs[axis]
            pltpu.make_async_remote_copy(
                buf.at[behind], buf.at[behind], self.send.at[base + d], self.recv.at[base + d],
                device_id=self.mate(axis, behind), device_id_type=MESH).wait_recv()
        total = self.bufs[axis][0]
        for k in range(1, self.sizes[axis]):
            total = total + self.bufs[axis][k]
        return total


def adam_step(grads, moment_one, moment_two, master):
    moment_one_new = 0.9 * moment_one + 0.1 * grads
    moment_two_new = 0.999 * moment_two + 0.001 * grads * grads
    first_hat = moment_one_new / (1.0 - 0.9**10)
    second_hat = moment_two_new / (1.0 - 0.999**10)
    master_new = master - 0.01 * (first_hat / (jnp.sqrt(second_hat) + 1e-08) + 0.1 * master)
    return moment_one_new, moment_two_new, master_new


def dot_exact(left, right):
    return lax.dot_general(left, right, NN, precision=lax.Precision.HIGHEST, preferred_element_type=f32)


def diagonals(block):
    row = lax.broadcasted_iota(jnp.int32, (128, 128), 0)
    lane = lax.broadcasted_iota(jnp.int32, (128, 128), 1)
    turned = dot_exact(block, (row + lane == 127).astype(f32))
    wide = jnp.concatenate([turned, jnp.zeros_like(turned)], axis=1)
    return jnp.sum(pltpu.roll(wide, 0, 1, stride=1, stride_axis=0), axis=0, keepdims=True)


def table_rows(diag, far, heads, buckets):
    tall = diag.shape[1]
    lane = lax.broadcasted_iota(jnp.int32, (tall, 128), 1)
    sums = jnp.where(lane == buckets // 2 - 1, jnp.sum(far[0], axis=1, keepdims=True), 0.0)
    sums = sums + jnp.where(lane == buckets - 1, jnp.sum(far[1], axis=1, keepdims=True), 0.0)
    for n in range(3):
        offset = lax.broadcasted_iota(jnp.int32, (256, 128), 0) - 127 + 128 * (n - 1)
        onehot = bucket_index(offset) == lax.broadcasted_iota(jnp.int32, (256, 128), 1)
        sums = sums + dot_exact(diag[n], onehot.astype(f32))
    found = []
    for t in range(heads * buckets // 128):
        place = lax.broadcasted_iota(jnp.int32, (128, 128), 1) + 128 * t
        bucket = lax.broadcasted_iota(jnp.int32, (128, 128), 0)
        spread = jnp.logical_and(place >= heads * bucket, place < heads * bucket + heads)
        wide = dot_exact(sums, spread.astype(f32))
        place = lax.broadcasted_iota(jnp.int32, (tall, 128), 1) + 128 * t
        head = place - heads * ((place * (65536 // heads + 1)) >> 16)
        mine = head == lax.broadcasted_iota(jnp.int32, (tall, 128), 0)
        found.append(jnp.sum(jnp.where(mine, wide, 0.0), axis=0, keepdims=True))
    return found


def back_kernel(grid, chunk, early, late, ends, spread, heads, buckets, *refs):
    (q_ref, k_ref, v_ref, gm_ref, mixed_ref, prob_ref, normed_ref, x_ref, ghid_ref, gain_ref, wq_ref, wk_ref, wv_ref,
     ggain_ref, m1_ref, m2_ref, ma_ref, flat_ref,
     gtok_out, gshard_out, m1_out, m2_out, ma_out, copy_out) = refs[:24]
    rest = refs[24:]
    taken = []
    for job in (early, late, ends, spread):
        size = len(job.scratch())
        taken.append(rest[:size])
        rest = rest[size:]
    (slope, gq, gk, gv, rk, rv, flat, wide, diag, far, gt_in, halo, halo_in, summed, renewed, fresh, ftail,
     lsem, s_kv, r_kv, s_turn, r_turn) = rest
    g = grid.here()
    step = pl.program_id(0)
    rows, width = normed_ref.shape
    keys = k_ref.shape[0]
    spans = rows // 128
    blocks = keys // 128 + spans - 1
    pairs = pl.num_programs(0) - 1
    first = spans - 1 + g.core * spans
    mate = g.device(core=1 - g.core)
    dp = lax.axis_index("dp")
    twin = (dp - g.core + g.y, g.core)
    moved = g.core != g.y
    count = grid.devices
    place = dp * 2 + g.y
    after = lax.rem(place + 1, count)
    nextdoor = (lax.div(after, 2), lax.rem(after, 2))
    before = lax.rem(place + count - 1, count)
    prior = (lax.div(before, 2), lax.rem(before, 2))
    shard = ma_ref.shape[0]
    stride, window = early.stride, early.window
    early.bind(flat_ref, summed.at[pl.ds(count, window), :], taken[0])
    late.bind(flat, summed.at[pl.ds(count, window), :], taken[1])
    ends.bind(taken[2])
    spread.bind(fresh, copy_out, taken[3])
    owner = g.plane >= early.first
    agenda = [(early, 1, k) for k in range(early.count)]
    split = early.count - 1
    jobs = [(early, k) for k in range(early.count)]
    jobs[split:split] = [(late, k) for k in range(late.count)]
    for n in range(len(jobs) + 1):
        agenda += [(job, stage, k) for stage, m in ((2, n), (3, n - 1)) if 0 <= m < len(jobs) for job, k in (jobs[m],)]
    square = width * width // 128
    over = flat.shape[0] - 3 * square
    edge = lambda: pltpu.make_async_copy(flat_ref.at[pl.ds(0, over), :], flat.at[pl.ds(3 * square, over), :], lsem.at[0])
    ghid_copy = lambda: pltpu.make_async_copy(ghid_ref, gtok_out, lsem.at[1])
    gt_copy = lambda: pltpu.make_async_remote_copy(
        gq, gt_in, s_turn.at[0], r_turn.at[0], device_id=twin, device_id_type=MESH)
    halo_copy = lambda: pltpu.make_async_remote_copy(
        halo, halo_in, s_turn.at[1], r_turn.at[1], device_id=nextdoor, device_id_type=MESH)

    def square_grad(right, base):
        third = width // 3
        for k in range(3):
            flatten_into(dot_of(normed_ref[:, third * k : third * k + third], right, TN), wide, flat, base + k * square // 3)

    @pl.when(step == 0)
    def _():
        barrier = pltpu.get_barrier_semaphore()
        partners = g.partners() + [prior, nextdoor]
        for one in partners:
            pl.semaphore_signal(barrier, inc=1, device_id=one, device_id_type=MESH)

        @pl.when(moved)
        def _():
            pl.semaphore_signal(barrier, inc=1, device_id=twin, device_id_type=MESH)

        pl.semaphore_wait(barrier, len(partners) + jnp.where(moved, 1, 0))
        edge().start()
        ghid_copy().start()
        for k in range(early.count):
            early.step(0, k)
        for k, state in enumerate((m1_ref, m2_ref, ma_ref)):
            halo[k] = state[pl.ds(shard - count, count), :]
        halo_copy().start()

    shares = [early.count * 2 // 6, early.count * 4 // 6, early.count * 5 // 6, early.count, early.count + 1]
    for n, (start, stop) in enumerate(zip([0] + shares[:-1], shares)):
        @pl.when(step == n + 1)
        def _():
            for job, stage, k in agenda[start:stop]:
                job.step(stage, k)

    pending = agenda[shares[-1] :]
    pending += [(late, 4 + level, k) for level in range(late.levels) for k in range(late.count)]

    def due(count, late_too=False):
        for _ in range(count):
            if pending and (late_too or pending[0][0] is early):
                job, stage, k = pending.pop(0)
                job.step(stage, k)

    @pl.when(step < pairs)
    def _():
        inner = (gm_ref[...].astype(f32) * mixed_ref[...].astype(f32)).T
        parts = ([], [], [])
        for head in range(2):
            row_inner = jnp.sum(inner[64 * head : 64 * head + 64], axis=0, keepdims=True)
            grown = gm_ref[...]
            grown = jnp.where(lane_mask(rows, head), grown, jnp.zeros_like(grown))
            for c in range(keys // chunk):
                part = pl.ds(chunk * c, chunk)
                back = dot_of(v_ref[part, :], grown, NT)
                slope[head, part, :] = (prob_ref[head, part, :].astype(f32) * (back - row_inner)).astype(bf16)
            parts[0].append(dot_of(k_ref[...], slope[head], TN))
            parts[1].append(dot_of(slope[head], q_ref[...], NN))
            parts[2].append(dot_of(prob_ref[head], gm_ref[...], NN))
            low = jnp.zeros((8, 128), f32)
            high = jnp.zeros((8, 128), f32)
            mids = [jnp.zeros((128, 128), f32) for _ in range(3)]
            for b in range(blocks):
                total = None
                for s in range(spans):
                    j = b - (spans - 1) + s
                    if 0 <= j < keys // 128:
                        term = slope[head, pl.ds(128 * j, 128), pl.ds(128 * s, 128)].astype(f32)
                        total = term if total is None else total + term
                wide[pl.ds(128 * b, 128), :] = total
                folded = total.reshape(16, 8, 128).sum(axis=0)
                low = low + jnp.where(b < first - 1, folded, 0.0)
                high = high + jnp.where(b > first + 1, folded, 0.0)
            line = pl.ds(2 * step + head, 1)
            for n in range(3):
                near = wide[pl.ds(pl.multiple_of(128 * (first - 1 + n), 128), 128), :]
                diag[n, line, :] = diagonals(near)
            far[0, line, :] = jnp.sum(low, axis=0, keepdims=True)
            far[1, line, :] = jnp.sum(high, axis=0, keepdims=True)
        lanes = pl.ds(pl.multiple_of(128 * step, 128), 128)
        gq[:, lanes] = jnp.concatenate([parts[0][0][:64], parts[0][1][64:]], axis=0).T.astype(bf16)
        mask = lane_mask(keys, 0)
        gk[:, lanes] = jnp.where(mask, parts[1][0], parts[1][1]).astype(bf16)
        gv[:, lanes] = jnp.where(mask, parts[2][0], parts[2][1]).astype(bf16)

    @pl.when(step == pairs)
    def _():
        mine = pl.ds(pl.multiple_of(g.core * rows, rows), rows)
        other = pl.ds(pl.multiple_of((1 - g.core) * rows, rows), rows)
        copies = [pltpu.make_async_remote_copy(a.at[other, :], b, s_kv.at[k], r_kv.at[k], device_id=mate, device_id_type=MESH)
                  for k, (a, b) in enumerate(((gk, rk), (gv, rv)))]
        for copy in copies:
            copy.start()
        square_grad(gq[...], 0)
        total = dot_of(gq[...], wq_ref[...], NT)
        due(1)
        for k, (a, b, w) in enumerate(((gk, rk, wk_ref), (gv, rv, wv_ref))):
            copies[k].wait()
            low = (a[mine, :].astype(f32) + b[...].astype(f32)).astype(bf16)
            b[...] = low
            square_grad(low, (k + 1) * square)
            total = total + dot_of(low, w[...], NT)
            due(2)
        edge().wait()
        for k in range(late.count):
            late.step(0, k)
        due(2)
        x = x_ref[...].astype(f32)
        scale = lax.rsqrt(jnp.mean(x * x, axis=1, keepdims=True) + 1e-06)
        unit = x * scale
        gain_row = jnp.sum(total * unit, axis=0, keepdims=True)
        c1 = total * gain_ref[...].astype(f32)
        ghid_copy().wait()
        gtok = gtok_out[...] + scale * (c1 - unit * jnp.mean(c1 * unit, axis=1, keepdims=True))
        gtok_out[...] = gtok

        @pl.when(moved)
        def _():
            gq[...] = gtok.astype(bf16)
            gt_copy().start()

        for k in range(late.count):
            late.step(1, k)
        due(2, True)

        tail = ends.mine(0)
        tail[...] = jnp.zeros(tail.shape, f32)
        for r in range(width // 128):
            tail[r : r + 1, :] = gain_row[:, 128 * r : 128 * r + 128]
            tail[width // 128 + r : width // 128 + r + 1, :] = ggain_ref[:, 128 * r : 128 * r + 128]
        for r, line in enumerate(table_rows(diag, far, heads, buckets)):
            tail[2 * width // 128 + r : 2 * width // 128 + r + 1, :] = line
        for k in range(3):
            tail[16 + k * count : 16 + (k + 1) * count, :] = jnp.where(place == count - 1, halo[k], 0.0)
        ends.start(0)
        for n in range(3):
            due(1, True)
            found = ends.done(n)
            ends.mine(n + 1)[...] = found
            ends.start(n + 1)
        due(len(pending), True)
        found = ends.done(3)
        grads = jnp.concatenate([found[:16], jnp.zeros((count - 16, 128), f32)], axis=0)
        last = [found[16 + k * count : 16 + (k + 1) * count] for k in range(3)]
        ftail[...] = adam_step(grads, *last)[2].astype(bf16)
        rest_copy = pltpu.make_async_copy(ftail, copy_out.at[pl.ds(stride * count, count), :], lsem.at[0])
        rest_copy.start()
        halo_copy().wait()
        summed[pl.ds(0, count), :] = jnp.zeros((count, 128), f32)

        def renew(job):
            job.collect()

            @pl.when(place == count - 1)
            def _():
                summed[pl.ds(count + stride, count), :] = grads

            renewed[pl.ds(0, count), :] = adam_step(summed[pl.ds(place, count), :], *[halo_in[k] for k in range(3)])[2]
            for start in range(0, shard, 216):
                size = min(216, shard - start)
                part = pl.ds(start, size)
                own = summed[pl.ds(place + count + start, size), :]
                one, two, new = adam_step(own, m1_ref[part, :], m2_ref[part, :], ma_ref[part, :])
                gshard_out[part, :] = own
                m1_out[part, :] = one
                m2_out[part, :] = two
                ma_out[part, :] = new
                renewed[pl.ds(count + start, size), :] = new
            for start in range(0, stride, stride // 8):
                fresh[pl.ds(start, stride // 8), :] = renewed[pl.ds(start + count - place, stride // 8), :].astype(bf16)

        own = range(spread.parts)

        def open_own():
            spread.begin()
            for k in own:
                spread.step(0, k)

        @pl.when(owner)
        def _():
            renew(early)

        @pl.when(jnp.logical_not(owner))
        def _():
            renew(late)

        open_own()
        for n in range(spread.count + 2):
            for stage in (0, 1, 2):
                k = n - stage
                if 0 <= k < spread.count and (stage, k) not in [(0, k) for k in own]:
                    spread.step(stage, k)
        early.finish()
        late.finish()
        spread.finish()
        rest_copy.wait()

        @pl.when(moved)
        def _():
            gt_copy().wait()
            gtok_out[...] = gt_in[...].astype(f32)


def back(grid, heads, buckets, query, keys_all, values_all, grad_mixed, mixed, prob, normed, x, grad_hidden, gain,
         wq, wk, wv, ggain, moment_one, moment_two, master, flat, collective_id):
    rows, width = query.shape
    span = keys_all.shape[0]
    pairs = width // 128
    shard = master.shape[0]
    count = grid.devices
    stride, window = shard - 1, shard - 1 + count
    cut = grid.planes // 4
    late_rows = 3 * width * width // 128
    early = Scatter(grid, cut, grid.planes - cut, stride, window, late_rows, False)
    late = Scatter(grid, 0, cut, stride, window, 0, True)
    spread = Gather(grid, stride)
    ends = TailSum(grid, 16 + 3 * count)
    at = lambda s: jnp.minimum(s, pairs - 1)
    tall = lambda n: pl.BlockSpec((n, 128), lambda s: (0, at(s)))
    dma = pltpu.SemaphoreType.DMA
    state = (shard, 128)
    return pl.pallas_call(
        functools.partial(back_kernel, grid, 256, early, late, ends, spread, heads, buckets),
        grid=(pairs + 1,),
        in_specs=[tall(rows), tall(span), tall(span), tall(rows), tall(rows),
                  pl.BlockSpec((2, span, rows), lambda s: (at(s), 0, 0)),
                  once((rows, width)), once((rows, width)), pl.BlockSpec(memory_space=pl.ANY), once((1, width)),
                  once((width, width)), once((width, width)), once((width, width)),
                  once((1, width)), once(state), once(state), once(state),
                  pl.BlockSpec(memory_space=pl.ANY)],
        out_specs=[once((rows, width)), once(state), once(state), once(state), once(state),
                   pl.BlockSpec(memory_space=pl.ANY)],
        out_shape=[jax.ShapeDtypeStruct(s, t) for s, t in (
            ((rows, width), f32), (state, f32), (state, f32), (state, f32), (state, f32),
            (((stride + 1) * count, 128), bf16))],
        scratch_shapes=early.scratch() + late.scratch() + ends.scratch() + spread.scratch() + [
            pltpu.VMEM((2, span, rows), bf16), pltpu.VMEM((rows, width), bf16),
            pltpu.VMEM((span, width), bf16), pltpu.VMEM((span, width), bf16),
            pltpu.VMEM((rows, width), bf16), pltpu.VMEM((rows, width), bf16),
            pltpu.VMEM((late_rows + count, 128), bf16), pltpu.VMEM((late_rows // 9, 128), f32),
            pltpu.VMEM((3, 16, 256), f32), pltpu.VMEM((2, 16, 128), f32),
            pltpu.VMEM((rows, width), bf16),
            pltpu.VMEM((3, count, 128), f32), pltpu.VMEM((3, count, 128), f32),
            pltpu.VMEM((count + window, 128), f32), pltpu.VMEM((count + shard + 7, 128), f32),
            pltpu.VMEM((stride, 128), bf16), pltpu.VMEM((count, 128), bf16),
            dma((2,)), dma((2,)), dma((2,)), dma((2,)), dma((2,))],
        compiler_params=pltpu.CompilerParams(collective_id=collective_id, has_side_effects=True, vmem_limit_bytes=62 << 20),
    )(query, keys_all, values_all, grad_mixed, mixed, prob, normed, x, grad_hidden, gain, wq, wk, wv, ggain,
      moment_one, moment_two, master, flat)


def per_device(tokens, lengths, cotangent, w_query, w_keys, w_values, w_output, w_gate, w_up, w_down,
               gain_attn, gain_ffn, bias_table, master, moment_one, moment_two):
    rows, width = tokens.shape
    grid = Grid(lax.axis_size("dp")).here()
    span = rows * lax.axis_size("group")
    count = grid.devices
    first_row = grid.core * rows
    near = near_rows(bias_table, rows, span, first_row)
    lens = jnp.broadcast_to(lengths.reshape(1, 1), (8, 128))
    gain_one, gain_two = gain_attn.reshape(1, width), gain_ffn.reshape(1, width)
    x, cot, lens, normed, query, keys_all, values_all, mixed, prob = front(
        grid, tokens, cotangent, lens, gain_one, w_query, w_keys, w_values, near, 1)
    layer_out, grad_hidden, grad_mixed, grad_gain_ffn, flat = ffn(
        lens, x, mixed, cot, gain_two, w_output, w_gate, w_up, w_down, count, 3)
    grad_tokens, grad_shard, moment_one_new, moment_two_new, master_new, fresh_copy = back(
        grid, bias_table.shape[1], bias_table.shape[0], query, keys_all, values_all, grad_mixed, mixed, prob, normed, x,
        grad_hidden, gain_one, w_query, w_keys, w_values, grad_gain_ffn, moment_one, moment_two, master, flat, 2)
    return (layer_out, grad_tokens, grad_shard, moment_one_new, moment_two_new, master_new, fresh_copy)


def solution(mesh):
    both = P(("dp", "group"), None)
    return jax.shard_map(
        per_device,
        mesh=mesh,
        in_specs=(both, P("dp"), both) + (P(),) * 10 + (both,) * 3,
        out_specs=(both,) * 6 + (P(),),
        check_vma=False,
    )
```
